32 devices in a mesh: dp: 8 (over z, core), expert: 4 (over y, x).
Axes of the slice: x: 2, y: 2, z: 4, core: 2. Of those that a mesh axis runs over, the one named last changes fastest.
Arguments:
- tokens: bfloat16 [4096, 2048], P(('dp', 'expert')), may hold values from -6 to 6
- expert_ids: int32 [4096, 4], P(('dp', 'expert')), may hold values from 0 to 7, as said below
- gate_weights: float32 [4096, 4], P(('dp', 'expert')), may hold values from 0.1 to 0.6
- hot_ids: int32 [2], replicated, may hold values from 0 to 7, as said below
- w_gate: bfloat16 [8, 2048, 768], P('expert', 'dp'), may hold values from -0.125 to 0.125
- w_up: bfloat16 [8, 2048, 768], P('expert', 'dp'), may hold values from -0.125 to 0.125
- w_down: bfloat16 [8, 768, 2048], P('expert', None, 'dp'), may hold values from -0.21875 to 0.21875
Outputs:
- moe_out: bfloat16 [4096, 2048], P(('dp', 'expert'))
The draws below stay inside these ranges and needn't reach their ends.
Inputs may be any that keep to these rules, and one draw needn't show every extreme that they name: `expert_ids`: tokens are in aligned blocks of 128 rows, one block a device. Column 0 of each row names an expert of hot_ids, each listed expert exactly 64 times in every block. Columns 1 to 3 name experts outside hot_ids, all different within a row; each such expert appears at most 128 times in a block, and one of them exactly 128 times in every block. `hot_ids`: the listed experts are all different, and one of them is expert 8 - 1.
All inputs are finite; a program needn't handle non-finite values.
Results may differ from the reference program's by a relative error of at most 0.0057.
Values may be sent and summed in bfloat16 or wider, within the bound.
No kernel may reach another device: no remote copies, remote signals or barrier semaphores. Data moves between devices by JAX's collectives and lax.ppermute only.
A program may use at most 384 MiB of HBM per device.

```python
import jax
import jax.numpy as jnp
from jax import lax

D = 2048
FF = 768
TOP = 4
HOT = 2
TOK_DEV = 128
EXPERTS = 8
TOKENS = 4096
CAP = 128
HCAP = 64


def route_tables(key):
    blocks = TOKENS // TOK_DEV
    cold_count = EXPERTS - HOT
    grid_count = cold_count * CAP
    pair_count = TOK_DEV * (TOP - 1)
    others = jax.random.permutation(jax.random.fold_in(key, 11), EXPERTS - 1).astype(jnp.int32)
    last_one = jnp.full((1,), EXPERTS - 1, jnp.int32)
    hot_drawn = jnp.concatenate([last_one, others[:HOT - 1]], axis=0)
    hot_order = jax.random.permutation(jax.random.fold_in(key, 17), HOT).astype(jnp.int32)
    hot_list = hot_drawn[hot_order]
    cold_list = others[HOT - 1:]

    def one_block(block_key):
        key_first = jax.random.fold_in(block_key, 1)
        key_grid = jax.random.fold_in(block_key, 2)
        key_second = jax.random.fold_in(block_key, 3)
        token_perm = jax.random.permutation(key_first, TOK_DEV).astype(jnp.int32)
        hot_column = jnp.zeros((TOK_DEV,), jnp.int32).at[token_perm].set(hot_list[jnp.arange(TOK_DEV, dtype=jnp.int32) % HOT])
        positions = jnp.arange(grid_count, dtype=jnp.int32)
        scores = jax.random.permutation(key_grid, grid_count).astype(jnp.int32) + grid_count
        scores = jnp.where(positions < CAP, positions, scores)
        picked_slots = jnp.sort(jnp.argsort(scores)[:pair_count].astype(jnp.int32))
        chosen = cold_list[picked_slots // CAP].reshape(TOP - 1, TOK_DEV)
        second_perm = jax.random.permutation(key_second, TOK_DEV).astype(jnp.int32)
        cold_columns = jnp.zeros((TOK_DEV, TOP - 1), jnp.int32).at[second_perm].set(chosen.T)
        return jnp.concatenate([hot_column[:, None], cold_columns], axis=1)
    block_keys = jax.random.split(jax.random.fold_in(key, 13), blocks)
    route_ids = jax.vmap(one_block)(block_keys).reshape(TOKENS, TOP)
    return (route_ids, hot_list)


def draw_expert_ids(key, part):
    route_ids, hot_list = route_tables(jax.random.fold_in(key, 5))
    return route_ids


def draw_hot_ids(key, part):
    route_ids, hot_list = route_tables(jax.random.fold_in(key, 5))
    return hot_list


def shard_levels(own_key, dims, pieces, smallest, top_value):
    gain = 1.0
    for dim, blocks in pieces:
        heights = jax.random.uniform(jax.random.fold_in(jax.random.fold_in(own_key, 6), dim), (blocks,), jnp.float32, smallest / len(pieces), top_value / len(pieces))
        gain = gain * jnp.repeat(jnp.exp(heights), dims[dim] // blocks).reshape((-1,) + (1,) * (len(dims) - 1 - dim))
    return gain


def bell_draw(own_key, shape, deviation, reach, pieces=(), kind=jnp.bfloat16):
    level = shard_levels(own_key, shape, pieces, -0.22, 0.18) if pieces else 1.0
    result = jax.random.normal(own_key, shape, jnp.float32) * deviation * level
    return jnp.minimum(jnp.maximum(result, -reach), reach).astype(kind)


def setup_inputs(seed: int = 0) -> dict:
    splits = jax.random.split(jax.random.key(seed), 8)
    tokens = bell_draw(splits[0], (TOKENS, D), 1.0, 6.0, ((0, 32),))
    expert_ids = draw_expert_ids(jax.random.fold_in(splits[7], 71), 0)
    gate_weights = jnp.clip(0.1 + 0.5 * jax.random.uniform(splits[2], (TOKENS, TOP), jnp.float32) ** shard_levels(splits[2], (TOKENS, TOP), ((0, 32),), -0.2, 0.2), 0.1, 0.6)
    hot_ids = draw_hot_ids(jax.random.fold_in(splits[7], 71), 0)
    w_gate = bell_draw(splits[4], (EXPERTS, D, FF), D ** -0.5, 0.125, ((0, 4), (1, 8)))
    w_up = bell_draw(splits[5], (EXPERTS, D, FF), D ** -0.5, 0.125, ((0, 4), (1, 8)))
    w_down = bell_draw(splits[6], (EXPERTS, FF, D), FF ** -0.5, 0.21875, ((0, 4), (2, 8)))
    return dict(tokens=tokens, expert_ids=expert_ids, gate_weights=gate_weights, hot_ids=hot_ids, w_gate=w_gate, w_up=w_up, w_down=w_down)


def expert_apply(row_block, gate_weight, up_weight, down_weight):
    gate_sum = jnp.dot(row_block, gate_weight, preferred_element_type=jnp.float32)
    up_sum = jnp.dot(row_block, up_weight, preferred_element_type=jnp.float32)
    hidden = (jax.nn.silu(gate_sum) * up_sum).astype(jnp.bfloat16)
    return jnp.dot(hidden, down_weight, preferred_element_type=jnp.float32).astype(jnp.bfloat16)


def routed(token_blocks, route_ids, gate_table, expert, slot_cap, gate_weight, up_weight, down_weight):
    blocks, tok_dev, model_width = token_blocks.shape
    slot_count = route_ids.shape[2]
    pair_count = tok_dev * slot_count
    flat_ids = route_ids.reshape(blocks, pair_count)
    flat_gates = gate_table.reshape(blocks, pair_count)
    is_hit = flat_ids == expert
    rank_index = jnp.cumsum(is_hit.astype(jnp.int32), axis=1).astype(jnp.int32) - 1
    slot_where = jnp.where(is_hit, rank_index, slot_cap).astype(jnp.int32)
    pair_index = jnp.broadcast_to(jnp.arange(pair_count, dtype=jnp.int32)[None, :], (blocks, pair_count))
    block_rows = jnp.broadcast_to(jnp.arange(blocks, dtype=jnp.int32)[:, None], (blocks, pair_count))
    slot_table = jnp.full((blocks, slot_cap + 1), pair_count, jnp.int32)
    slot_table = slot_table.at[block_rows, slot_where].set(pair_index)[:, :slot_cap]
    token_index = (slot_table // slot_count).astype(jnp.int32)
    gates_padded = jnp.concatenate([flat_gates, jnp.zeros((blocks, 1), jnp.float32)], axis=1)
    weighting = jnp.take_along_axis(gates_padded, slot_table, axis=1)
    padded = jnp.concatenate([token_blocks, jnp.zeros((blocks, 1, model_width), jnp.bfloat16)], axis=1)
    block_index = jnp.arange(blocks, dtype=jnp.int32)[:, None]
    row_block = padded[block_index, token_index]
    expert_out = expert_apply(row_block.reshape(blocks * slot_cap, model_width), gate_weight, up_weight, down_weight)
    contribution = expert_out.reshape(blocks, slot_cap, model_width).astype(jnp.float32) * weighting[:, :, None]
    accum_sum = jnp.zeros((blocks, tok_dev + 1, model_width), jnp.float32)
    accum_sum = accum_sum.at[block_index, token_index].add(contribution)
    return accum_sum[:, :tok_dev]


def reference(tokens, expert_ids, gate_weights, hot_ids, w_gate, w_up, w_down):
    blocks = TOKENS // TOK_DEV
    token_blocks = tokens.reshape(blocks, TOK_DEV, D)
    route_ids = expert_ids.reshape(blocks, TOK_DEV, TOP)
    gate_table = gate_weights.reshape(blocks, TOK_DEV, TOP)

    def cold_step(accum_sum, scan_item):
        gate_weight, up_weight, down_weight, expert = scan_item
        term = routed(token_blocks, route_ids[:, :, 1:], gate_table[:, :, 1:], expert, CAP, gate_weight, up_weight, down_weight)
        return accum_sum + term, None

    accum_sum = jnp.zeros((blocks, TOK_DEV, D), jnp.float32)
    accum_sum, _ = lax.scan(cold_step, accum_sum, (w_gate, w_up, w_down, jnp.arange(EXPERTS, dtype=jnp.int32)))

    def hot_step(accum_sum, expert):
        term = routed(token_blocks, route_ids[:, :, :1], gate_table[:, :, :1], expert, HCAP, w_gate[expert], w_up[expert], w_down[expert])
        return accum_sum + term, None

    accum_sum, _ = lax.scan(hot_step, accum_sum, hot_ids)
    return accum_sum.reshape(TOKENS, D).astype(jnp.bfloat16)
```

```python
import functools

import jax
import jax.numpy as jnp
from jax import lax
from jax.experimental import pallas as pl
from jax.experimental.pallas import tpu as pltpu
from jax.sharding import PartitionSpec as P

LANES = 128
VMEM = 56 * 1024 * 1024


def gate_columns(expert_ids, gate_weights, experts):
    named = expert_ids[:, :, None] == jnp.arange(experts, dtype=jnp.int32)
    table = jnp.sum(jnp.where(named, gate_weights[:, :, None], 0.0), axis=1)
    parts = []
    rest = table
    for _ in range(3):
        part = lax.reduce_precision(rest, 8, 7)
        parts.append(part.astype(jnp.bfloat16))
        rest = rest - part
    packed = jnp.concatenate(parts, axis=1)
    width = -(-packed.shape[1] // LANES) * LANES
    return jnp.pad(packed, ((0, 0), (0, width - packed.shape[1])))


def hidden_kernel(slices, offsets_ref, rows_ref, *refs):
    gate_up, hidden_ref = refs[:slices], refs[slices]
    depth, both = gate_up[0].shape
    sums = jnp.zeros((rows_ref.shape[0], both), jnp.float32)
    for k in range(slices):
        columns = pl.ds(pl.multiple_of(offsets_ref[k], LANES), depth)
        sums += jnp.dot(rows_ref[:, columns], gate_up[k][...], preferred_element_type=jnp.float32)
    gate_sum, up_sum = sums[:, : both // 2], sums[:, both // 2 :]
    hidden_ref[...] = (gate_sum / (1.0 + jnp.exp(-gate_sum)) * up_sum).astype(jnp.bfloat16)


def hidden_of(rows, gate_up, offsets):
    count, width = rows.shape
    both = gate_up[0].shape[1]
    block = min(count, 512)
    return pl.pallas_call(
        functools.partial(hidden_kernel, len(gate_up)),
        grid=(count // block,),
        in_specs=[pl.BlockSpec(memory_space=pltpu.SMEM), pl.BlockSpec((block, width), lambda i: (i, 0))]
        + [pl.BlockSpec(w.shape, lambda i: (0, 0)) for w in gate_up],
        out_specs=pl.BlockSpec((block, both // 2), lambda i: (i, 0)),
        out_shape=jax.ShapeDtypeStruct((count, both // 2), jnp.bfloat16),
        compiler_params=pltpu.CompilerParams(vmem_limit_bytes=VMEM),
        cost_estimate=pl.CostEstimate(
            flops=2 * count * width * both, bytes_accessed=2 * width * (count + both), transcendentals=count * both // 2
        ),
    )(offsets, rows, *gate_up)


def down_kernel(slices, experts, offsets_ref, hidden_ref, gates_ref, *refs):
    down, out_ref = refs[:slices], refs[slices]
    lane = lax.broadcasted_iota(jnp.int32, gates_ref.shape, 1)
    expert = offsets_ref[slices]
    chosen = (lane < 3 * experts) & (lax.rem(lane, experts) == expert)
    gate = jnp.sum(jnp.where(chosen, gates_ref[...].astype(jnp.float32), 0.0), axis=1, keepdims=True)
    hidden = hidden_ref[...]
    for k in range(slices):
        part = jnp.dot(hidden, down[k][...], preferred_element_type=jnp.float32)
        part = part.astype(jnp.bfloat16).astype(jnp.float32) * gate
        columns = pl.ds(pl.multiple_of(offsets_ref[k], LANES), down[k].shape[1])
        out_ref[:, columns] = part.astype(jnp.bfloat16)


def outputs_of(hidden, rows, down, offsets, experts):
    count, inner = hidden.shape
    depth = down[0].shape[1]
    model = depth * len(down)
    extra = rows.shape[1] - model
    block = min(count, 512)
    return pl.pallas_call(
        functools.partial(down_kernel, len(down), experts),
        grid=(count // block,),
        in_specs=[
            pl.BlockSpec(memory_space=pltpu.SMEM),
            pl.BlockSpec((block, inner), lambda i: (i, 0)),
            pl.BlockSpec((block, extra), lambda i: (i, model // extra)),
        ]
        + [pl.BlockSpec(w.shape, lambda i: (0, 0)) for w in down],
        out_specs=pl.BlockSpec((block, model), lambda i: (i, 0)),
        out_shape=jax.ShapeDtypeStruct((count, model), jnp.bfloat16),
        compiler_params=pltpu.CompilerParams(vmem_limit_bytes=VMEM),
        cost_estimate=pl.CostEstimate(
            flops=2 * count * model * inner, bytes_accessed=2 * model * (count + inner), transcendentals=0
        ),
    )(offsets, hidden, rows, *down)


def shards(tokens, expert_ids, gate_weights, hot_ids, w_gate, w_up, w_down):
    del hot_ids
    tok_rows, model = tokens.shape
    places, lines = lax.axis_size("expert"), lax.axis_size("dp")
    layers = lines // 2
    half = layers // 2
    experts = places * w_gate.shape[0]
    depth = w_gate.shape[1]

    def swap_layer(array, mask):
        return lax.ppermute(array, "dp", [(i, i ^ (2 * mask)) for i in range(lines)])

    def swap_core(array):
        return lax.ppermute(array, "dp", [(i, i ^ 1) for i in range(lines)])

    def swap_place(array, mask):
        return lax.ppermute(array, "expert", [(i, i ^ mask) for i in range(places)])

    mirror = layers - 1
    line = lax.axis_index("dp")
    side = (line >= lines // 2).astype(jnp.int32)
    here = lax.axis_index("expert") * w_gate.shape[0] + side

    def pick(array, which):
        return lax.dynamic_index_in_dim(array, which, 0, keepdims=False)

    block = jnp.concatenate([tokens, gate_columns(expert_ids, gate_weights, experts)], axis=1)
    far_block = swap_layer(block, mirror)
    gate_up = jnp.concatenate([w_gate, w_up], axis=2)

    def spread(array):
        own = pick(array, side)
        far = swap_layer(pick(array, 1 - side), mirror)
        near = [(0, own), (mirror, far)]
        for mask in range(1, half):
            near.append((mask, swap_layer(own, mask)))
            near.append((mask ^ mirror, swap_layer(far, mask)))
        found = [(2 * mask, piece) for mask, piece in near]
        found += [(2 * mask + 1, swap_core(piece)) for mask, piece in near]
        return found

    def gather_places(rows):
        mask = 1
        while mask < places:
            rows = jnp.concatenate([rows, swap_place(rows, mask)], axis=0)
            mask *= 2
        return rows

    def home(parts):
        total = parts[:tok_rows].astype(jnp.float32)
        for mask in range(1, places):
            total += swap_place(parts[mask * tok_rows : (mask + 1) * tok_rows], mask).astype(jnp.float32)
        return total

    gate_up_found = spread(gate_up)
    down_found = spread(w_down)
    offsets = jnp.stack([(line ^ mask) * depth for mask, _ in gate_up_found] + [here]).astype(jnp.int32)
    gate_up_list = [piece for _, piece in gate_up_found]
    down_list = [piece for _, piece in down_found]

    rows, far_rows = gather_places(block), gather_places(far_block)
    far_hidden = hidden_of(far_rows, gate_up_list, offsets)
    far_parts = outputs_of(far_hidden, far_rows, down_list, offsets, experts)
    far_sum = swap_layer(home(far_parts).astype(jnp.bfloat16), mirror)
    hidden = hidden_of(rows, gate_up_list, offsets)
    parts = outputs_of(hidden, rows, down_list, offsets, experts)
    return (home(parts) + far_sum.astype(jnp.float32)).astype(jnp.bfloat16)


def solution(mesh):
    placed = (
        P(("dp", "expert"), None),
        P(("dp", "expert"), None),
        P(("dp", "expert"), None),
        P(),
        P("expert", "dp", None),
        P("expert", "dp", None),
        P("expert", None, "dp"),
    )
    return jax.shard_map(
        shards, mesh=mesh, in_specs=placed, out_specs=P(("dp", "expert"), None), check_vma=False
    )
```

```python
import functools

import jax
import jax.numpy as jnp
from jax import lax
from jax.experimental import pallas as pl
from jax.experimental.pallas import tpu as pltpu
from jax.sharding import PartitionSpec as P

LANES = 128
VMEM = 62 * 1024 * 1024
FREE = pl.CostEstimate(flops=0, bytes_accessed=0, transcendentals=0)
ANY = pl.BlockSpec(memory_space=pl.ANY)
SMEM = pl.BlockSpec(memory_space=pltpu.SMEM)


def gate_columns(expert_ids, gate_weights, experts):
    named = expert_ids[:, :, None] == jnp.arange(experts, dtype=jnp.int32)
    table = jnp.sum(jnp.where(named, gate_weights[:, :, None], 0.0), axis=1)
    parts = []
    rest = table
    for _ in range(3):
        part = lax.reduce_precision(rest, 8, 7)
        parts.append(part.astype(jnp.bfloat16))
        rest = rest - part
    packed = jnp.concatenate(parts, axis=1)
    width = -(-packed.shape[1] // LANES) * LANES
    return jnp.pad(packed, ((0, 0), (0, width - packed.shape[1])))


def after(array, *earlier):
    return lax.optimization_barrier((array, *earlier))[0]


class Loads:
    def __init__(self, sems):
        self.sems, self.used = sems, 0

    def add(self, source, target):
        self.used += 1
        return pltpu.make_async_copy(source, target, self.sems.at[self.used - 1])


def row_loads(loads, row_refs, rows, numbers_ref, slices, depth):
    tok_rows, span = row_refs[0].shape[0], 4 * depth
    copies = []
    for j in range(slices // 4):
        columns = pl.ds(pl.multiple_of(numbers_ref[slices + j], LANES), span)
        for b, row_ref in enumerate(row_refs):
            target = rows.at[pl.ds(b * tok_rows, tok_rows), pl.ds(j * span, span)]
            copies.append(loads.add(row_ref.at[:, columns], target))
    return copies


def weight_loads(loads, weight_refs, weights, numbers_ref, tiles, tile):
    depth, both = weight_refs[0].shape
    copies = []
    for t in range(tiles):
        copies.append([])
        for k, weight_ref in enumerate(weight_refs):
            place = pl.ds(pl.multiple_of((k // 4) * 4 * depth + numbers_ref[k], LANES), depth)
            for part in range(2):
                source = weight_ref.at[:, pl.ds(part * (both // 2) + t * tile, tile)]
                target = weights.at[t, place, pl.ds(part * tile, tile)]
                copies[t].append(loads.add(source, target))
    return copies


def early_kernel(blocks, slices, numbers_ref, *refs):
    row_refs, refs = refs[:blocks], refs[blocks:]
    weight_refs, (gate_out, up_out, rows, weights, sems) = refs[:slices], refs[slices:]
    tiles, _, twice = weights.shape
    tile = twice // 2
    step = pl.program_id(0)
    loads = Loads(sems)
    first = row_loads(loads, row_refs, rows, numbers_ref, slices, weight_refs[0].shape[0])
    by_tile = weight_loads(loads, weight_refs, weights, numbers_ref, tiles, tile)

    @pl.when(step == 0)
    def _():
        for copy in first + [copy for copies in by_tile for copy in copies]:
            copy.start()
        for copy in first:
            copy.wait()

    for t in range(tiles):

        @pl.when(step == t)
        def _():
            for copy in by_tile[t]:
                copy.wait()
            sums = jnp.dot(rows[...], weights[t], preferred_element_type=jnp.float32)
            gate_out[...] = sums[:, :tile]
            up_out[...] = sums[:, tile:]


def late_kernel(blocks, slices, down_slices, experts, model, numbers_ref, *refs):
    row_refs, refs = refs[:blocks], refs[blocks:]
    weight_refs, refs = refs[:slices], refs[slices:]
    down_refs, refs = refs[:down_slices], refs[down_slices:]
    gate_in, up_in, hidden_out, refs = refs[0], refs[1], refs[2], refs[3:]
    out_refs, (rows, weights, hidden, down, gates, sems) = refs[:blocks], refs[blocks:]
    tok_rows = row_refs[0].shape[0]
    tiles, _, twice = weights.shape
    tile = twice // 2
    step = pl.program_id(0)
    loads = Loads(sems)
    first = row_loads(loads, row_refs, rows, numbers_ref, slices, weight_refs[0].shape[0])
    by_tile = weight_loads(loads, weight_refs, weights, numbers_ref, tiles, tile)
    final = [loads.add(ref, down.at[k]) for k, ref in enumerate(down_refs)]
    for b, row_ref in enumerate(row_refs):
        source = row_ref.at[:, pl.ds(model, gates.shape[1])]
        final.append(loads.add(source, gates.at[pl.ds(b * tok_rows, tok_rows)]))

    @pl.when(step == 0)
    def _():
        for copy in first + [copy for copies in by_tile for copy in copies] + final:
            copy.start()
        for copy in first:
            copy.wait()

    for t in range(tiles):

        @pl.when(step == t)
        def _():
            for copy in by_tile[t]:
                copy.wait()
            sums = jnp.dot(rows[...], weights[t], preferred_element_type=jnp.float32)
            gate_sum = sums[:, :tile] + gate_in[...]
            up_sum = sums[:, tile:] + up_in[...]
            hidden[:, t * tile : (t + 1) * tile] = (gate_sum / (1.0 + jnp.exp(-gate_sum)) * up_sum).astype(jnp.bfloat16)

    @pl.when(step == tiles - 1)
    def _():
        for copy in final:
            copy.wait()
        first_down = slices + slices // 4
        weigh_out(hidden, [down.at[k] for k in range(down_slices)], gates, out_refs, experts, numbers_ref, first_down)
        hidden_out[...] = hidden[...]


def weigh_out(hidden, down, gates, out_refs, experts, numbers_ref, at):
    tok_rows = out_refs[0].shape[0]
    lane = lax.broadcasted_iota(jnp.int32, gates.shape, 1)
    chosen = (lane < 3 * experts) & (lax.rem(lane, experts) == numbers_ref[at + len(down)])
    gate = jnp.sum(jnp.where(chosen, gates[...].astype(jnp.float32), 0.0), axis=1, keepdims=True)
    for k, weights in enumerate(down):
        part = jnp.dot(hidden[...], weights[...], preferred_element_type=jnp.float32)
        part = (part.astype(jnp.bfloat16).astype(jnp.float32) * gate).astype(jnp.bfloat16)
        columns = pl.ds(pl.multiple_of(numbers_ref[at + k], LANES), part.shape[1])
        for b, out_ref in enumerate(out_refs):
            out_ref[:, columns] = part[b * tok_rows : (b + 1) * tok_rows]


def early_sums(row_blocks, gate_up, numbers):
    blocks, slices = len(row_blocks), len(gate_up)
    depth, both = gate_up[0].shape
    count, inner = blocks * row_blocks[0].shape[0], both // 2
    tile = 256 if inner % 256 == 0 else inner
    tiles = inner // tile
    spec = pl.BlockSpec((count, tile), lambda i: (0, i))
    return pl.pallas_call(
        functools.partial(early_kernel, blocks, slices),
        grid=(tiles,),
        in_specs=[SMEM] + [ANY] * (blocks + slices),
        out_specs=[spec, spec],
        out_shape=[jax.ShapeDtypeStruct((count, inner), jnp.float32)] * 2,
        scratch_shapes=[
            pltpu.VMEM((count, slices * depth), jnp.bfloat16),
            pltpu.VMEM((tiles, slices * depth, 2 * tile), jnp.bfloat16),
            pltpu.SemaphoreType.DMA((slices // 4 * blocks + 2 * tiles * slices,)),
        ],
        compiler_params=pltpu.CompilerParams(vmem_limit_bytes=VMEM),
        cost_estimate=FREE,
    )(numbers, *row_blocks, *gate_up)


def late_outputs(row_blocks, gate_up, down, numbers, early, experts):
    blocks, slices, down_slices = len(row_blocks), len(gate_up), len(down)
    depth, both = gate_up[0].shape
    tok_rows, width = row_blocks[0].shape
    extra = -(-3 * experts // LANES) * LANES
    count, inner = blocks * tok_rows, both // 2
    tile = 256 if inner % 256 == 0 else inner
    tiles = inner // tile
    spec = pl.BlockSpec((count, tile), lambda i: (0, i))
    out = (tok_rows, down_slices * depth)
    results = pl.pallas_call(
        functools.partial(late_kernel, blocks, slices, down_slices, experts, width - extra),
        grid=(tiles,),
        in_specs=[SMEM] + [ANY] * (blocks + slices + down_slices) + [spec, spec],
        out_specs=[pl.BlockSpec((count, inner), lambda i: (0, 0))] + [pl.BlockSpec(out, lambda i: (0, 0))] * blocks,
        out_shape=[jax.ShapeDtypeStruct((count, inner), jnp.bfloat16)] + [jax.ShapeDtypeStruct(out, jnp.bfloat16)] * blocks,
        scratch_shapes=[
            pltpu.VMEM((count, slices * depth), jnp.bfloat16),
            pltpu.VMEM((tiles, slices * depth, 2 * tile), jnp.bfloat16),
            pltpu.VMEM((count, inner), jnp.bfloat16),
            pltpu.VMEM((down_slices, inner, depth), jnp.bfloat16),
            pltpu.VMEM((count, extra), jnp.bfloat16),
            pltpu.SemaphoreType.DMA((slices // 4 * blocks + 2 * tiles * slices + down_slices + blocks,)),
        ],
        compiler_params=pltpu.CompilerParams(vmem_limit_bytes=VMEM),
        cost_estimate=FREE,
    )(numbers, *row_blocks, *gate_up, *down, *early)
    return results[0], results[1:]


def down_kernel(blocks, slices, experts, model, numbers_ref, hidden_ref, *refs):
    row_refs, refs = refs[:blocks], refs[blocks:]
    weight_refs, refs = refs[:slices], refs[slices:]
    out_refs, (gates, sems) = refs[:blocks], refs[blocks:]
    tok_rows = row_refs[0].shape[0]
    loads = Loads(sems)
    copies = []
    for b, row_ref in enumerate(row_refs):
        source = row_ref.at[:, pl.ds(model, gates.shape[1])]
        copies.append(loads.add(source, gates.at[pl.ds(b * tok_rows, tok_rows)]))
    for copy in copies:
        copy.start()
    for copy in copies:
        copy.wait()
    weigh_out(hidden_ref, weight_refs, gates, out_refs, experts, numbers_ref, 0)


def outputs_of(hidden, row_blocks, down, offsets, experts):
    blocks, slices = len(row_blocks), len(down)
    count, inner = hidden.shape
    depth = down[0].shape[1]
    tok_rows = row_blocks[0].shape[0]
    extra = -(-3 * experts // LANES) * LANES
    model = row_blocks[0].shape[1] - extra
    whole = pl.BlockSpec(memory_space=pltpu.VMEM)
    return pl.pallas_call(
        functools.partial(down_kernel, blocks, slices, experts, model),
        in_specs=[SMEM, whole] + [ANY] * blocks + [whole] * slices,
        out_specs=[whole] * blocks,
        out_shape=[jax.ShapeDtypeStruct((tok_rows, slices * depth), jnp.bfloat16)] * blocks,
        scratch_shapes=[pltpu.VMEM((count, extra), jnp.bfloat16), pltpu.SemaphoreType.DMA((blocks,))],
        compiler_params=pltpu.CompilerParams(vmem_limit_bytes=VMEM),
        cost_estimate=FREE,
    )(offsets, hidden, *row_blocks, *down)


def finish_kernel(mine, bases_ref, *refs):
    parts, sums, out_ref = refs[:mine], refs[mine:-1], refs[-1]
    for group, ref in enumerate(sums):
        columns = pl.ds(pl.multiple_of(bases_ref[group], LANES), ref.shape[1])
        total = ref[...].astype(jnp.float32)
        for part in parts:
            total += part[:, columns].astype(jnp.float32)
        out_ref[:, columns] = total.astype(jnp.bfloat16)


def shards(tokens, expert_ids, gate_weights, hot_ids, w_gate, w_up, w_down):
    del hot_ids
    tok_rows, model = tokens.shape
    places, lines = lax.axis_size("expert"), lax.axis_size("dp")
    layers = lines // 2
    half = layers // 2
    mirror = layers - 1
    local_count, depth = w_gate.shape[:2]
    experts = places * local_count
    assert local_count == 2 and half % 2 == 0

    def swap_layer(array, mask):
        return lax.ppermute(array, "dp", [(i, i ^ (2 * mask)) for i in range(lines)])

    def swap_core(array):
        return lax.ppermute(array, "dp", [(i, i ^ 1) for i in range(lines)])

    def swap_place(array, mask):
        return lax.ppermute(array, "expert", [(i, i ^ mask) for i in range(places)])

    line = lax.axis_index("dp")
    layer = line // 2
    parity = lax.rem(layer, 2)
    side = line // (lines // 2)
    here = lax.axis_index("expert") * local_count + side
    near, away = list(range(half)), list(range(half, layers))

    def pick(array, which):
        return lax.dynamic_index_in_dim(array, which, 0, keepdims=False)

    def numbers(values):
        return jnp.stack([jnp.asarray(v, jnp.int32) for v in values])

    def lines_of(masks):
        return [line ^ (2 * mask + core) for mask in masks for core in range(2)]

    def places_of(masks):
        first = [(layer - parity) ^ mask for mask in masks[::2]]
        return numbers([lax.rem(v, 4) * depth for v in lines_of(masks)] + [2 * v * depth for v in first])

    def both_cores(found, found_core, masks):
        return [piece for mask in masks for piece in (found[mask], found_core[mask])]

    block = jnp.concatenate([tokens, gate_columns(expert_ids, gate_weights, experts)], axis=1)
    far_block = swap_layer(block, mirror)
    own = [block] + [swap_place(block, mask) for mask in range(1, places)]

    singles = [1 << i for i in range(places.bit_length() - 1)]
    ready = after(side, block)
    mine, theirs = [jnp.concatenate([pick(w_gate, which), pick(w_up, which)], axis=1) for which in (ready, 1 - ready)]
    dn_mine, dn_theirs = pick(w_down, side), pick(w_down, 1 - side)
    gu, dn = {0: mine}, {0: dn_mine}
    for mask in near[1:]:
        gu[mask] = swap_layer(mine, mask)
    gu[mirror] = swap_layer(after(theirs, far_block, *[own[mask] for mask in singles]), mirror)
    far = [far_block] + [swap_place(after(far_block, own[mask]), mask) for mask in range(1, places)]
    for mask in near[1:]:
        dn[mask] = swap_layer(after(dn_mine, gu[mask]), mask)
    gu_core = {mask: swap_core(gu[mask]) for mask in near}
    pieces = both_cores(gu, gu_core, near)
    chunks = {"far": [far[i : i + 4] for i in range(0, places, 4)], "own": [own[i : i + 4] for i in range(0, places, 4)]}
    early = {"own": [early_sums(chunk, pieces, places_of(near)) for chunk in chunks["own"]]}
    settled = [*own[1:], *far[1:], *[dn[mask] for mask in near], *[sums for pair in early["own"] for sums in pair]]
    for mask in near[1:]:
        gu[mask ^ mirror] = swap_layer(after(gu[mirror], gu[mask], *settled), mask)
    dn[mirror] = swap_layer(after(dn_theirs, gu[mirror]), mirror)
    early["far"] = [early_sums(chunk, pieces, places_of(near)) for chunk in chunks["far"]]
    dn_core = {mask: swap_core(dn[mask]) for mask in near}
    settled = [sums for pair in early["far"] for sums in pair] + [dn_core[mask] for mask in near] + [dn[mirror]]
    for mask in away:
        gu_core[mask] = swap_core(after(gu[mask], *(settled if mask != mirror else ())))

    def arrived(parts):
        return [parts[0]] + [swap_place(parts[mask], mask) for mask in range(1, places)]

    def add_up(parts):
        total = parts[0].astype(jnp.float32)
        for part in parts[1:]:
            total += part.astype(jnp.float32)
        return total.astype(jnp.bfloat16)

    def late(key, masks):
        columns = [lax.rem(v, 2 * len(masks)) * depth for v in lines_of(masks)]
        counted = jnp.concatenate([places_of(away), numbers(columns + [here])])
        hidden, parts = [], []
        for chunk, sums in zip(chunks[key], early[key]):
            pieces = both_cores(gu, gu_core, away)
            rows, blocks = late_outputs(chunk, pieces, both_cores(dn, dn_core, masks), counted, sums, experts)
            hidden.append(rows)
            parts += blocks
        return hidden, parts

    far_hidden, far_parts = late("far", near)
    for mask in near[1:]:
        dn[mask ^ mirror] = swap_layer(after(dn[mirror], gu[mask ^ mirror], *[dn_core[other] for other in near]), mask)
    for mask in away:
        dn_core[mask] = swap_core(after(dn[mask], far_hidden[-1]))
    starts = numbers([lax.rem(v, 2 * len(away)) * depth for v in lines_of(away)] + [here])
    more_parts = []
    for chunk, rows in zip(chunks["far"], far_hidden):
        more_parts += outputs_of(rows, chunk, both_cores(dn, dn_core, away), starts, experts)
    sums = [swap_layer(add_up(arrived(parts)), mirror) for parts in (far_parts, more_parts)]
    mine = arrived(late("own", near + away)[1])
    width = model // 2
    bases = numbers([(1 - side) * width, side * width])
    whole = pl.BlockSpec(memory_space=pltpu.VMEM)
    return pl.pallas_call(
        functools.partial(finish_kernel, len(mine)),
        in_specs=[SMEM] + [whole] * (len(mine) + len(sums)),
        out_specs=whole,
        out_shape=jax.ShapeDtypeStruct((tok_rows, model), jnp.bfloat16),
        compiler_params=pltpu.CompilerParams(vmem_limit_bytes=VMEM),
    )(bases, *mine, *sums)


def solution(mesh):
    placed = (
        P(("dp", "expert"), None),
        P(("dp", "expert"), None),
        P(("dp", "expert"), None),
        P(),
        P("expert", "dp", None),
        P("expert", "dp", None),
        P("expert", None, "dp"),
    )
    return jax.shard_map(
        shards, mesh=mesh, in_specs=placed, out_specs=P(("dp", "expert"), None), check_vma=False
    )
```

```python
import functools

import jax
import jax.numpy as jnp
from jax import lax
from jax.experimental import pallas as pl
from jax.experimental.pallas import tpu as pltpu
from jax.sharding import PartitionSpec as P

LANES = 128
VMEM = 62 * 1024 * 1024
FREE = pl.CostEstimate(flops=0, bytes_accessed=0, transcendentals=0)
ANY = pl.BlockSpec(memory_space=pl.ANY)
SMEM = pl.BlockSpec(memory_space=pltpu.SMEM)


def gate_columns(expert_ids, gate_weights, experts):
    named = expert_ids[:, :, None] == jnp.arange(experts, dtype=jnp.int32)
    table = jnp.sum(jnp.where(named, gate_weights[:, :, None], 0.0), axis=1)
    parts = []
    rest = table
    for _ in range(3):
        part = lax.reduce_precision(rest, 8, 7)
        parts.append(part.astype(jnp.bfloat16))
        rest = rest - part
    packed = jnp.concatenate(parts, axis=1)
    width = -(-packed.shape[1] // LANES) * LANES
    return jnp.pad(packed, ((0, 0), (0, width - packed.shape[1])))


def after(array, *earlier):
    return lax.optimization_barrier((array, *earlier))[0]


class Loads:
    def __init__(self, sems):
        self.sems, self.used = sems, 0

    def add(self, source, target):
        self.used += 1
        return pltpu.make_async_copy(source, target, self.sems.at[self.used - 1])


def row_loads(loads, row_refs, rows, numbers_ref, slices, depth):
    tok_rows, span = row_refs[0].shape[0], 4 * depth
    copies = []
    for j in range(slices // 4):
        columns = pl.ds(pl.multiple_of(numbers_ref[slices + j], LANES), span)
        for b, row_ref in enumerate(row_refs):
            target = rows.at[pl.ds(b * tok_rows, tok_rows), pl.ds(j * span, span)]
            copies.append(loads.add(row_ref.at[:, columns], target))
    return copies


def weight_loads(loads, weight_refs, weights, numbers_ref, tiles, tile):
    depth, both = weight_refs[0].shape
    copies = []
    for t in range(tiles):
        copies.append([])
        for k, weight_ref in enumerate(weight_refs):
            place = pl.ds(pl.multiple_of((k // 4) * 4 * depth + numbers_ref[k], LANES), depth)
            for part in range(2):
                source = weight_ref.at[:, pl.ds(part * (both // 2) + t * tile, tile)]
                target = weights.at[t, place, pl.ds(part * tile, tile)]
                copies[t].append(loads.add(source, target))
    return copies


def early_kernel(blocks, slices, numbers_ref, *refs):
    row_refs, refs = refs[:blocks], refs[blocks:]
    weight_refs, (gate_out, up_out, rows, weights, sems) = refs[:slices], refs[slices:]
    tiles, _, twice = weights.shape
    tile = twice // 2
    step = pl.program_id(0)
    loads = Loads(sems)
    first = row_loads(loads, row_refs, rows, numbers_ref, slices, weight_refs[0].shape[0])
    by_tile = weight_loads(loads, weight_refs, weights, numbers_ref, tiles, tile)

    @pl.when(step == 0)
    def _():
        for copy in first + [copy for copies in by_tile for copy in copies]:
            copy.start()
        for copy in first:
            copy.wait()

    for t in range(tiles):

        @pl.when(step == t)
        def _():
            for copy in by_tile[t]:
                copy.wait()
            sums = jnp.dot(rows[...], weights[t], preferred_element_type=jnp.float32)
            gate_out[...] = sums[:, :tile]
            up_out[...] = sums[:, tile:]


def late_kernel(blocks, slices, down_slices, experts, model, numbers_ref, *refs):
    row_refs, refs = refs[:blocks], refs[blocks:]
    weight_refs, refs = refs[:slices], refs[slices:]
    down_refs, refs = refs[:down_slices], refs[down_slices:]
    gate_in, up_in, hidden_out, refs = refs[0], refs[1], refs[2], refs[3:]
    out_refs, (rows, weights, hidden, down, gates, sems) = refs[:blocks], refs[blocks:]
    tok_rows = row_refs[0].shape[0]
    tiles, _, twice = weights.shape
    tile = twice // 2
    step = pl.program_id(0)
    loads = Loads(sems)
    first = row_loads(loads, row_refs, rows, numbers_ref, slices, weight_refs[0].shape[0])
    by_tile = weight_loads(loads, weight_refs, weights, numbers_ref, tiles, tile)
    final = [loads.add(ref, down.at[k]) for k, ref in enumerate(down_refs)]
    for b, row_ref in enumerate(row_refs):
        source = row_ref.at[:, pl.ds(model, gates.shape[1])]
        final.append(loads.add(source, gates.at[pl.ds(b * tok_rows, tok_rows)]))

    @pl.when(step == 0)
    def _():
        for copy in first + [copy for copies in by_tile for copy in copies] + final:
            copy.start()
        for copy in first:
            copy.wait()

    for t in range(tiles):

        @pl.when(step == t)
        def _():
            for copy in by_tile[t]:
                copy.wait()
            sums = jnp.dot(rows[...], weights[t], preferred_element_type=jnp.float32)
            gate_sum = sums[:, :tile] + gate_in[...]
            up_sum = sums[:, tile:] + up_in[...]
            hidden[:, t * tile : (t + 1) * tile] = (gate_sum / (1.0 + jnp.exp(-gate_sum)) * up_sum).astype(jnp.bfloat16)

    @pl.when(step == tiles - 1)
    def _():
        for copy in final:
            copy.wait()
        first_down = slices + slices // 4
        weigh_out(hidden, [down.at[k] for k in range(down_slices)], gates, out_refs, experts, numbers_ref, first_down)
        hidden_out[...] = hidden[...]


def weigh_out(hidden, down, gates, out_refs, experts, numbers_ref, at):
    tok_rows = out_refs[0].shape[0]
    lane = lax.broadcasted_iota(jnp.int32, gates.shape, 1)
    chosen = (lane < 3 * experts) & (lax.rem(lane, experts) == numbers_ref[at + len(down)])
    gate = jnp.sum(jnp.where(chosen, gates[...].astype(jnp.float32), 0.0), axis=1, keepdims=True)
    for k, weights in enumerate(down):
        part = jnp.dot(hidden[...], weights[...], preferred_element_type=jnp.float32)
        part = (part.astype(jnp.bfloat16).astype(jnp.float32) * gate).astype(jnp.bfloat16)
        columns = pl.ds(pl.multiple_of(numbers_ref[at + k], LANES), part.shape[1])
        for b, out_ref in enumerate(out_refs):
            out_ref[:, columns] = part[b * tok_rows : (b + 1) * tok_rows]


def early_sums(row_blocks, gate_up, numbers):
    blocks, slices = len(row_blocks), len(gate_up)
    depth, both = gate_up[0].shape
    count, inner = blocks * row_blocks[0].shape[0], both // 2
    tile = 256 if inner % 256 == 0 else inner
    tiles = inner // tile
    spec = pl.BlockSpec((count, tile), lambda i: (0, i))
    return pl.pallas_call(
        functools.partial(early_kernel, blocks, slices),
        grid=(tiles,),
        in_specs=[SMEM] + [ANY] * (blocks + slices),
        out_specs=[spec, spec],
        out_shape=[jax.ShapeDtypeStruct((count, inner), jnp.float32)] * 2,
        scratch_shapes=[
            pltpu.VMEM((count, slices * depth), jnp.bfloat16),
            pltpu.VMEM((tiles, slices * depth, 2 * tile), jnp.bfloat16),
            pltpu.SemaphoreType.DMA((slices // 4 * blocks + 2 * tiles * slices,)),
        ],
        compiler_params=pltpu.CompilerParams(vmem_limit_bytes=VMEM),
        cost_estimate=FREE,
    )(numbers, *row_blocks, *gate_up)


def late_outputs(row_blocks, gate_up, down, numbers, early, experts):
    blocks, slices, down_slices = len(row_blocks), len(gate_up), len(down)
    depth, both = gate_up[0].shape
    tok_rows, width = row_blocks[0].shape
    extra = -(-3 * experts // LANES) * LANES
    count, inner = blocks * tok_rows, both // 2
    tile = 256 if inner % 256 == 0 else inner
    tiles = inner // tile
    spec = pl.BlockSpec((count, tile), lambda i: (0, i))
    out = (tok_rows, down_slices * depth)
    results = pl.pallas_call(
        functools.partial(late_kernel, blocks, slices, down_slices, experts, width - extra),
        grid=(tiles,),
        in_specs=[SMEM] + [ANY] * (blocks + slices + down_slices) + [spec, spec],
        out_specs=[pl.BlockSpec((count, inner), lambda i: (0, 0))] + [pl.BlockSpec(out, lambda i: (0, 0))] * blocks,
        out_shape=[jax.ShapeDtypeStruct((count, inner), jnp.bfloat16)] + [jax.ShapeDtypeStruct(out, jnp.bfloat16)] * blocks,
        scratch_shapes=[
            pltpu.VMEM((count, slices * depth), jnp.bfloat16),
            pltpu.VMEM((tiles, slices * depth, 2 * tile), jnp.bfloat16),
            pltpu.VMEM((count, inner), jnp.bfloat16),
            pltpu.VMEM((down_slices, inner, depth), jnp.bfloat16),
            pltpu.VMEM((count, extra), jnp.bfloat16),
            pltpu.SemaphoreType.DMA((slices // 4 * blocks + 2 * tiles * slices + down_slices + blocks,)),
        ],
        compiler_params=pltpu.CompilerParams(vmem_limit_bytes=VMEM),
        cost_estimate=FREE,
    )(numbers, *row_blocks, *gate_up, *down, *early)
    return results[0], results[1:]


def down_kernel(blocks, slices, experts, model, numbers_ref, hidden_ref, *refs):
    row_refs, refs = refs[:blocks], refs[blocks:]
    weight_refs, refs = refs[:slices], refs[slices:]
    out_refs, (gates, sems) = refs[:blocks], refs[blocks:]
    tok_rows = row_refs[0].shape[0]
    loads = Loads(sems)
    copies = []
    for b, row_ref in enumerate(row_refs):
        source = row_ref.at[:, pl.ds(model, gates.shape[1])]
        copies.append(loads.add(source, gates.at[pl.ds(b * tok_rows, tok_rows)]))
    for copy in copies:
        copy.start()
    for copy in copies:
        copy.wait()
    weigh_out(hidden_ref, weight_refs, gates, out_refs, experts, numbers_ref, 0)


def outputs_of(hidden, row_blocks, down, offsets, experts):
    blocks, slices = len(row_blocks), len(down)
    count, inner = hidden.shape
    depth = down[0].shape[1]
    tok_rows = row_blocks[0].shape[0]
    extra = -(-3 * experts // LANES) * LANES
    model = row_blocks[0].shape[1] - extra
    whole = pl.BlockSpec(memory_space=pltpu.VMEM)
    return pl.pallas_call(
        functools.partial(down_kernel, blocks, slices, experts, model),
        in_specs=[SMEM, whole] + [ANY] * blocks + [whole] * slices,
        out_specs=[whole] * blocks,
        out_shape=[jax.ShapeDtypeStruct((tok_rows, slices * depth), jnp.bfloat16)] * blocks,
        scratch_shapes=[pltpu.VMEM((count, extra), jnp.bfloat16), pltpu.SemaphoreType.DMA((blocks,))],
        compiler_params=pltpu.CompilerParams(vmem_limit_bytes=VMEM),
        cost_estimate=FREE,
    )(offsets, hidden, *row_blocks, *down)


def finish_kernel(mine, bases_ref, *refs):
    parts, sums, out_ref = refs[:mine], refs[mine:-1], refs[-1]
    for group, ref in enumerate(sums):
        columns = pl.ds(pl.multiple_of(bases_ref[group], LANES), ref.shape[1])
        total = ref[...].astype(jnp.float32)
        for part in parts:
            total += part[:, columns].astype(jnp.float32)
        out_ref[:, columns] = total.astype(jnp.bfloat16)


def shards(tokens, expert_ids, gate_weights, hot_ids, w_gate, w_up, w_down):
    del hot_ids
    tok_rows, model = tokens.shape
    places, lines = lax.axis_size("expert"), lax.axis_size("dp")
    layers = lines // 2
    half = layers // 2
    mirror = layers - 1
    local_count, depth = w_gate.shape[:2]
    experts = places * local_count
    assert local_count == 2 and half % 2 == 0

    def swap_layer(array, mask):
        return lax.ppermute(array, "dp", [(i, i ^ (2 * mask)) for i in range(lines)])

    def swap_core(array):
        return lax.ppermute(array, "dp", [(i, i ^ 1) for i in range(lines)])

    def swap_place(array, mask):
        return lax.ppermute(array, "expert", [(i, i ^ mask) for i in range(places)])

    line = lax.axis_index("dp")
    layer = line // 2
    parity = lax.rem(layer, 2)
    side = line // (lines // 2)
    here = lax.axis_index("expert") * local_count + side
    near, away = list(range(half)), list(range(half, layers))

    def pick(array, which):
        return lax.dynamic_index_in_dim(array, which, 0, keepdims=False)

    def numbers(values):
        return jnp.stack([jnp.asarray(v, jnp.int32) for v in values])

    def lines_of(masks):
        return [line ^ (2 * mask + core) for mask in masks for core in range(2)]

    def places_of(masks):
        first = [(layer - parity) ^ mask for mask in masks[::2]]
        return numbers([lax.rem(v, 4) * depth for v in lines_of(masks)] + [2 * v * depth for v in first])

    def both_cores(found, found_core, masks):
        return [piece for mask in masks for piece in (found[mask], found_core[mask])]

    singles = [1 << i for i in range(places.bit_length() - 1)]
    others = [mask for mask in range(1, places) if mask not in singles]
    block = jnp.concatenate([tokens, gate_columns(expert_ids, gate_weights, experts)], axis=1)
    dn = {0: pick(w_down, side)}
    far = {0: swap_layer(block, mirror)}
    own = {0: block, **{mask: swap_place(block, mask) for mask in range(1, places)}}
    for mask in near[1:]:
        dn[mask] = swap_layer(dn[0], mask)
    wave = [far[0], *[own[mask] for mask in singles], *[dn[mask] for mask in near[1:]]]

    mine, theirs = [jnp.concatenate([pick(w_gate, which), pick(w_up, which)], axis=1) for which in (side, 1 - side)]
    gu = {0: mine, mirror: swap_layer(after(theirs, *wave), mirror)}
    for mask in near[1:]:
        gu[mask] = swap_layer(after(mine, *wave), mask)
    for mask in singles:
        far[mask] = swap_place(after(far[0], *wave), mask)
    for mask in others:
        far[mask] = swap_place(after(far[0], *wave), mask)
    wave = [gu[mirror], *[gu[mask] for mask in near[1:]], *[far[mask] for mask in range(1, places)], *[own[mask] for mask in others]]

    for mask in near[1:]:
        gu[mask ^ mirror] = swap_layer(after(gu[mirror], *wave), mask)
    dn[mirror] = swap_layer(after(pick(w_down, 1 - side), *wave), mirror)
    gu_core = {mask: swap_core(after(gu[mask], *wave)) for mask in near + [mirror]}
    pieces = both_cores(gu, gu_core, near)
    chunks = {}
    for key, found in (("far", far), ("own", own)):
        blocks = [found[mask] for mask in range(places)]
        chunks[key] = [blocks[i : i + 4] for i in range(0, places, 4)]
    early = {key: [early_sums(chunk, pieces, places_of(near)) for chunk in chunks[key]] for key in ("own", "far")}
    settled = {key: [sums for pair in early[key] for sums in pair] for key in early}
    dn_core = {mask: swap_core(after(dn[mask], *settled["own"])) for mask in near}
    wave = [*settled["far"], *[dn_core[mask] for mask in near], dn[mirror]]
    for mask in near[1:]:
        gu_core[mask ^ mirror] = swap_core(after(gu[mask ^ mirror], *wave))

    def arrived(parts):
        return [parts[0]] + [swap_place(parts[mask], mask) for mask in range(1, places)]

    def add_up(parts):
        total = parts[0].astype(jnp.float32)
        for part in parts[1:]:
            total += part.astype(jnp.float32)
        return total.astype(jnp.bfloat16)

    def late(key, masks):
        columns = [lax.rem(v, 2 * len(masks)) * depth for v in lines_of(masks)]
        counted = jnp.concatenate([places_of(away), numbers(columns + [here])])
        hidden, parts = [], []
        for chunk, sums in zip(chunks[key], early[key]):
            pieces = both_cores(gu, gu_core, away)
            rows, blocks = late_outputs(chunk, pieces, both_cores(dn, dn_core, masks), counted, sums, experts)
            hidden.append(rows)
            parts += blocks
        return hidden, parts

    far_hidden, far_parts = late("far", near)
    for mask in near[1:]:
        dn[mask ^ mirror] = swap_layer(after(dn[mirror], gu[mask ^ mirror], *[dn_core[other] for other in near]), mask)
    for mask in away:
        dn_core[mask] = swap_core(after(dn[mask], far_hidden[-1]))
    starts = numbers([lax.rem(v, 2 * len(away)) * depth for v in lines_of(away)] + [here])
    more_parts = []
    for chunk, rows in zip(chunks["far"], far_hidden):
        more_parts += outputs_of(rows, chunk, both_cores(dn, dn_core, away), starts, experts)
    sums = [swap_layer(add_up(arrived(parts)), mirror) for parts in (far_parts, more_parts)]
    mine = arrived(late("own", near + away)[1])
    width = model // 2
    bases = numbers([(1 - side) * width, side * width])
    whole = pl.BlockSpec(memory_space=pltpu.VMEM)
    return pl.pallas_call(
        functools.partial(finish_kernel, len(mine)),
        in_specs=[SMEM] + [whole] * (len(mine) + len(sums)),
        out_specs=whole,
        out_shape=jax.ShapeDtypeStruct((tok_rows, model), jnp.bfloat16),
        compiler_params=pltpu.CompilerParams(vmem_limit_bytes=VMEM),
    )(bases, *mine, *sums)


def solution(mesh):
    placed = (
        P(("dp", "expert"), None),
        P(("dp", "expert"), None),
        P(("dp", "expert"), None),
        P(),
        P("expert", "dp", None),
        P("expert", "dp", None),
        P("expert", None, "dp"),
    )
    return jax.shard_map(
        shards, mesh=mesh, in_specs=placed, out_specs=P(("dp", "expert"), None), check_vma=False
    )
```

```python
import functools

import jax
import jax.numpy as jnp
from jax import lax
from jax.experimental import pallas as pl
from jax.experimental.pallas import tpu as pltpu
from jax.sharding import PartitionSpec as P

LANES = 128
VMEM = 62 * 1024 * 1024
FREE = pl.CostEstimate(flops=0, bytes_accessed=0, transcendentals=0)
ANY = pl.BlockSpec(memory_space=pl.ANY)
SMEM = pl.BlockSpec(memory_space=pltpu.SMEM)


def gate_columns(expert_ids, gate_weights, experts):
    named = expert_ids[:, :, None] == jnp.arange(experts, dtype=jnp.int32)
    table = jnp.sum(jnp.where(named, gate_weights[:, :, None], 0.0), axis=1)
    parts = []
    rest = table
    for _ in range(3):
        part = lax.reduce_precision(rest, 8, 7)
        parts.append(part.astype(jnp.bfloat16))
        rest = rest - part
    packed = jnp.concatenate(parts, axis=1)
    width = -(-packed.shape[1] // LANES) * LANES
    return jnp.pad(packed, ((0, 0), (0, width - packed.shape[1])))


def after(array, *earlier):
    return lax.optimization_barrier((array, *earlier))[0]


class Loads:
    def __init__(self, sems):
        self.sems, self.used = sems, 0

    def add(self, source, target):
        self.used += 1
        return pltpu.make_async_copy(source, target, self.sems.at[self.used - 1])


def row_loads(loads, row_refs, rows, numbers_ref, slices, depth):
    tok_rows, span = row_refs[0].shape[0], 2 * depth
    copies = []
    for j in range(slices // 2):
        columns = pl.ds(pl.multiple_of(numbers_ref[slices + j], LANES), span)
        for b, row_ref in enumerate(row_refs):
            target = rows.at[pl.ds(b * tok_rows, tok_rows), pl.ds(j * span, span)]
            copies.append(loads.add(row_ref.at[:, columns], target))
    return copies


def weight_loads(loads, weight_refs, weights, numbers_ref, tiles, tile):
    depth, both = weight_refs[0].shape
    copies = []
    for t in range(tiles):
        copies.append([])
        for k, weight_ref in enumerate(weight_refs):
            place = pl.ds(pl.multiple_of(numbers_ref[k], LANES), depth)
            for part in range(2):
                source = weight_ref.at[:, pl.ds(part * (both // 2) + t * tile, tile)]
                target = weights.at[t, place, pl.ds(part * tile, tile)]
                copies[t].append(loads.add(source, target))
    return copies


def early_kernel(blocks, slices, numbers_ref, *refs):
    row_refs, refs = refs[:blocks], refs[blocks:]
    weight_refs, (gate_out, up_out, rows, weights, sems) = refs[:slices], refs[slices:]
    tiles, _, twice = weights.shape
    tile = twice // 2
    step = pl.program_id(0)
    loads = Loads(sems)
    first = row_loads(loads, row_refs, rows, numbers_ref, slices, weight_refs[0].shape[0])
    by_tile = weight_loads(loads, weight_refs, weights, numbers_ref, tiles, tile)

    @pl.when(step == 0)
    def _():
        for copy in first + [copy for copies in by_tile for copy in copies]:
            copy.start()
        for copy in first:
            copy.wait()

    for t in range(tiles):

        @pl.when(step == t)
        def _():
            for copy in by_tile[t]:
                copy.wait()
            sums = jnp.dot(rows[...], weights[t], preferred_element_type=jnp.float32)
            gate_out[...] = sums[:, :tile]
            up_out[...] = sums[:, tile:]


def late_kernel(blocks, slices, down_slices, experts, model, numbers_ref, *refs):
    row_refs, refs = refs[:blocks], refs[blocks:]
    weight_refs, refs = refs[:slices], refs[slices:]
    down_refs, refs = refs[:down_slices], refs[down_slices:]
    gate_in, up_in, hidden_out, refs = refs[0], refs[1], refs[2], refs[3:]
    out_refs, (rows, weights, hidden, down, gates, sems) = refs[:blocks], refs[blocks:]
    tok_rows = row_refs[0].shape[0]
    tiles, _, twice = weights.shape
    tile = twice // 2
    step = pl.program_id(0)
    loads = Loads(sems)
    first = row_loads(loads, row_refs, rows, numbers_ref, slices, weight_refs[0].shape[0])
    by_tile = weight_loads(loads, weight_refs, weights, numbers_ref, tiles, tile)
    final = [loads.add(ref, down.at[k]) for k, ref in enumerate(down_refs)]
    for b, row_ref in enumerate(row_refs):
        source = row_ref.at[:, pl.ds(model, gates.shape[1])]
        final.append(loads.add(source, gates.at[pl.ds(b * tok_rows, tok_rows)]))

    @pl.when(step == 0)
    def _():
        for copy in first + [copy for copies in by_tile for copy in copies] + final:
            copy.start()
        for copy in first:
            copy.wait()

    for t in range(tiles):

        @pl.when(step == t)
        def _():
            for copy in by_tile[t]:
                copy.wait()
            sums = jnp.dot(rows[...], weights[t], preferred_element_type=jnp.float32)
            gate_sum = sums[:, :tile] + gate_in[...]
            up_sum = sums[:, tile:] + up_in[...]
            hidden[:, t * tile : (t + 1) * tile] = (gate_sum / (1.0 + jnp.exp(-gate_sum)) * up_sum).astype(jnp.bfloat16)

    @pl.when(step == tiles - 1)
    def _():
        for copy in final:
            copy.wait()
        first_down = slices + slices // 2
        weigh_out(hidden, [down.at[k] for k in range(down_slices)], gates, out_refs, experts, numbers_ref, first_down)
        hidden_out[...] = hidden[...]


def weigh_out(hidden, down, gates, out_refs, experts, numbers_ref, at):
    tok_rows = out_refs[0].shape[0]
    lane = lax.broadcasted_iota(jnp.int32, gates.shape, 1)
    chosen = (lane < 3 * experts) & (lax.rem(lane, experts) == numbers_ref[at + len(down)])
    gate = jnp.sum(jnp.where(chosen, gates[...].astype(jnp.float32), 0.0), axis=1, keepdims=True)
    for k, weights in enumerate(down):
        part = jnp.dot(hidden[...], weights[...], preferred_element_type=jnp.float32)
        part = (part.astype(jnp.bfloat16).astype(jnp.float32) * gate).astype(jnp.bfloat16)
        columns = pl.ds(pl.multiple_of(numbers_ref[at + k], LANES), part.shape[1])
        for b, out_ref in enumerate(out_refs):
            out_ref[:, columns] = part[b * tok_rows : (b + 1) * tok_rows]


def early_sums(row_blocks, gate_up, numbers):
    blocks, slices = len(row_blocks), len(gate_up)
    depth, both = gate_up[0].shape
    count, inner = blocks * row_blocks[0].shape[0], both // 2
    tile = 256 if inner % 256 == 0 else inner
    tiles = inner // tile
    spec = pl.BlockSpec((count, tile), lambda i: (0, i))
    return pl.pallas_call(
        functools.partial(early_kernel, blocks, slices),
        grid=(tiles,),
        in_specs=[SMEM] + [ANY] * (blocks + slices),
        out_specs=[spec, spec],
        out_shape=[jax.ShapeDtypeStruct((count, inner), jnp.float32)] * 2,
        scratch_shapes=[
            pltpu.VMEM((count, slices * depth), jnp.bfloat16),
            pltpu.VMEM((tiles, slices * depth, 2 * tile), jnp.bfloat16),
            pltpu.SemaphoreType.DMA((slices // 2 * blocks + 2 * tiles * slices,)),
        ],
        compiler_params=pltpu.CompilerParams(vmem_limit_bytes=62 * 1024 * 1024),
        cost_estimate=FREE,
    )(numbers, *row_blocks, *gate_up)


def late_outputs(row_blocks, gate_up, down, numbers, early, experts):
    blocks, slices, down_slices = len(row_blocks), len(gate_up), len(down)
    depth, both = gate_up[0].shape
    tok_rows, width = row_blocks[0].shape
    extra = -(-3 * experts // LANES) * LANES
    count, inner = blocks * tok_rows, both // 2
    tile = 256 if inner % 256 == 0 else inner
    tiles = inner // tile
    spec = pl.BlockSpec((count, tile), lambda i: (0, i))
    out = (tok_rows, down_slices * depth)
    results = pl.pallas_call(
        functools.partial(late_kernel, blocks, slices, down_slices, experts, width - extra),
        grid=(tiles,),
        in_specs=[SMEM] + [ANY] * (blocks + slices + down_slices) + [spec, spec],
        out_specs=[pl.BlockSpec((count, inner), lambda i: (0, 0))] + [pl.BlockSpec(out, lambda i: (0, 0))] * blocks,
        out_shape=[jax.ShapeDtypeStruct((count, inner), jnp.bfloat16)] + [jax.ShapeDtypeStruct(out, jnp.bfloat16)] * blocks,
        scratch_shapes=[
            pltpu.VMEM((count, slices * depth), jnp.bfloat16),
            pltpu.VMEM((tiles, slices * depth, 2 * tile), jnp.bfloat16),
            pltpu.VMEM((count, inner), jnp.bfloat16),
            pltpu.VMEM((down_slices, inner, depth), jnp.bfloat16),
            pltpu.VMEM((count, extra), jnp.bfloat16),
            pltpu.SemaphoreType.DMA((slices // 2 * blocks + 2 * tiles * slices + down_slices + blocks,)),
        ],
        compiler_params=pltpu.CompilerParams(vmem_limit_bytes=62 * 1024 * 1024),
        cost_estimate=FREE,
    )(numbers, *row_blocks, *gate_up, *down, *early)
    return results[0], results[1:]


def down_kernel(blocks, slices, experts, model, numbers_ref, hidden_ref, *refs):
    row_refs, refs = refs[:blocks], refs[blocks:]
    weight_refs, refs = refs[:slices], refs[slices:]
    out_refs, (gates, sems) = refs[:blocks], refs[blocks:]
    tok_rows = row_refs[0].shape[0]
    loads = Loads(sems)
    copies = []
    for b, row_ref in enumerate(row_refs):
        source = row_ref.at[:, pl.ds(model, gates.shape[1])]
        copies.append(loads.add(source, gates.at[pl.ds(b * tok_rows, tok_rows)]))
    for copy in copies:
        copy.start()
    for copy in copies:
        copy.wait()
    weigh_out(hidden_ref, weight_refs, gates, out_refs, experts, numbers_ref, 0)


def outputs_of(hidden, row_blocks, down, offsets, experts):
    blocks, slices = len(row_blocks), len(down)
    count, inner = hidden.shape
    depth = down[0].shape[1]
    tok_rows = row_blocks[0].shape[0]
    extra = -(-3 * experts // LANES) * LANES
    model = row_blocks[0].shape[1] - extra
    whole = pl.BlockSpec(memory_space=pltpu.VMEM)
    return pl.pallas_call(
        functools.partial(down_kernel, blocks, slices, experts, model),
        in_specs=[SMEM, whole] + [ANY] * blocks + [whole] * slices,
        out_specs=[whole] * blocks,
        out_shape=[jax.ShapeDtypeStruct((tok_rows, slices * depth), jnp.bfloat16)] * blocks,
        scratch_shapes=[pltpu.VMEM((count, extra), jnp.bfloat16), pltpu.SemaphoreType.DMA((blocks,))],
        compiler_params=pltpu.CompilerParams(vmem_limit_bytes=24 * 1024 * 1024),
        cost_estimate=FREE,
    )(offsets, hidden, *row_blocks, *down)


def finish_kernel(mine, bases_ref, *refs):
    parts, sums, out_ref = refs[:mine], refs[mine:-1], refs[-1]
    for group, ref in enumerate(sums):
        columns = pl.ds(pl.multiple_of(bases_ref[group], LANES), ref.shape[1])
        total = ref[...].astype(jnp.float32)
        for part in parts:
            total += part[:, columns].astype(jnp.float32)
        out_ref[:, columns] = total.astype(jnp.bfloat16)


def shards(tokens, expert_ids, gate_weights, hot_ids, w_gate, w_up, w_down):
    del hot_ids
    tok_rows, model = tokens.shape
    places, lines = lax.axis_size("expert"), lax.axis_size("dp")
    layers = lines // 2
    half = layers // 2
    mirror = layers - 1
    local_count, depth = w_gate.shape[:2]
    experts = places * local_count
    assert local_count == 2 and half % 2 == 0

    def swap_layer(array, mask):
        return lax.ppermute(array, "dp", [(i, i ^ (2 * mask)) for i in range(lines)])

    def swap_core(array):
        return lax.ppermute(array, "dp", [(i, i ^ 1) for i in range(lines)])

    def swap_place(array, mask):
        return lax.ppermute(array, "expert", [(i, i ^ mask) for i in range(places)])

    line = lax.axis_index("dp")
    layer = line // 2
    parity = lax.rem(layer, 2)
    side = line // (lines // 2)
    here = lax.axis_index("expert") * local_count + side
    near, away = list(range(half)), list(range(half, layers))
    soon, last = near + [mirror], away[:-1]

    def pick(array, which):
        return lax.dynamic_index_in_dim(array, which, 0, keepdims=False)

    def numbers(values):
        return jnp.stack([jnp.asarray(v, jnp.int32) for v in values])

    def lines_of(masks):
        return [line ^ (2 * mask + core) for mask in masks for core in range(2)]

    def places_of(masks):
        first = [2 * (layer ^ mask) * depth for mask in masks]
        return numbers([(2 * (k // 2) + lax.rem(v, 2)) * depth for k, v in enumerate(lines_of(masks))] + first)

    def both_cores(found, found_core, masks):
        return [piece for mask in masks for piece in (found[mask], found_core[mask])]

    singles = [1 << i for i in range(places.bit_length() - 1)]
    others = [mask for mask in range(1, places) if mask not in singles]
    block = jnp.concatenate([tokens, gate_columns(expert_ids, gate_weights, experts)], axis=1)
    dn = {0: pick(w_down, side)}
    far = {0: swap_layer(block, mirror)}
    own = {0: block, **{mask: swap_place(block, mask) for mask in range(1, places)}}
    for mask in near[1:]:
        dn[mask] = swap_layer(dn[0], mask)
    wave = [far[0], *[own[mask] for mask in singles], *[dn[mask] for mask in near[1:]]]
    first = [far[0], *[dn[mask] for mask in near[1:]]]

    mine, theirs = [jnp.concatenate([pick(w_gate, which), pick(w_up, which)], axis=1) for which in (side, 1 - side)]
    gu = {0: mine, mirror: swap_layer(after(theirs, *first), mirror)}
    for mask in near[1:]:
        gu[mask] = swap_layer(after(mine, *first), mask)
    for mask in singles:
        far[mask] = swap_place(after(far[0], *wave), mask)
    for mask in others:
        far[mask] = swap_place(after(far[0], *wave), mask)
    wave = [gu[mirror], *[gu[mask] for mask in near[1:]], *[far[mask] for mask in range(1, places)], *[own[mask] for mask in others]]

    for mask in near[1:]:
        gu[mask ^ mirror] = swap_layer(after(gu[mirror], *wave), mask)
    dn[mirror] = swap_layer(after(pick(w_down, 1 - side), *wave), mirror)
    gu_core = {mask: swap_core(after(gu[mask], *wave)) for mask in near + [mirror]}
    pieces = both_cores(gu, gu_core, soon)
    chunks = {}
    for key, found in (("far", far), ("own", own)):
        blocks = [found[mask] for mask in range(places)]
        chunks[key] = [blocks[i : i + 4] for i in range(0, places, 4)]
    early = {key: [early_sums(chunk, pieces, places_of(soon)) for chunk in chunks[key]] for key in ("own", "far")}
    settled = {key: [sums for pair in early[key] for sums in pair] for key in early}
    dn_core = {mask: swap_core(after(dn[mask], *settled["own"])) for mask in near}
    wave = [*settled["far"], *[dn_core[mask] for mask in near], dn[mirror]]
    for mask in near[1:]:
        gu_core[mask ^ mirror] = swap_core(after(gu[mask ^ mirror], *wave))

    def arrived(parts):
        return [parts[0]] + [swap_place(parts[mask], mask) for mask in range(1, places)]

    def add_up(parts):
        total = parts[0].astype(jnp.float32)
        for part in parts[1:]:
            total += part.astype(jnp.float32)
        return total.astype(jnp.bfloat16)

    def late(key, masks):
        columns = [lax.rem(v, 2 * len(masks)) * depth for v in lines_of(masks)]
        counted = jnp.concatenate([places_of(last), numbers(columns + [here])])
        hidden, parts = [], []
        for chunk, sums in zip(chunks[key], early[key]):
            pieces = both_cores(gu, gu_core, last)
            rows, blocks = late_outputs(chunk, pieces, both_cores(dn, dn_core, masks), counted, sums, experts)
            hidden.append(rows)
            parts += blocks
        return hidden, parts

    far_hidden, far_parts = late("far", near)
    for mask in near[1:]:
        dn[mask ^ mirror] = swap_layer(after(dn[mirror], gu[mask ^ mirror], *[dn_core[other] for other in near]), mask)
    for mask in away:
        dn_core[mask] = swap_core(after(dn[mask], far_hidden[-1]))
    starts = numbers([lax.rem(v, 2 * len(away)) * depth for v in lines_of(away)] + [here])
    more_parts = []
    for chunk, rows in zip(chunks["far"], far_hidden):
        more_parts += outputs_of(rows, chunk, both_cores(dn, dn_core, away), starts, experts)
    sums = [swap_layer(add_up(arrived(parts)), mirror) for parts in (far_parts, more_parts)]
    mine = arrived(late("own", near + away)[1])
    width = model // 2
    bases = numbers([(1 - side) * width, side * width])
    whole = pl.BlockSpec(memory_space=pltpu.VMEM)
    return pl.pallas_call(
        functools.partial(finish_kernel, len(mine)),
        in_specs=[SMEM] + [whole] * (len(mine) + len(sums)),
        out_specs=whole,
        out_shape=jax.ShapeDtypeStruct((tok_rows, model), jnp.bfloat16),
        compiler_params=pltpu.CompilerParams(vmem_limit_bytes=16 * 1024 * 1024),
    )(bases, *mine, *sums)


def solution(mesh):
    placed = (
        P(("dp", "expert"), None),
        P(("dp", "expert"), None),
        P(("dp", "expert"), None),
        P(),
        P("expert", "dp", None),
        P("expert", "dp", None),
        P("expert", None, "dp"),
    )
    return jax.shard_map(
        shards, mesh=mesh, in_specs=placed, out_specs=P(("dp", "expert"), None), check_vma=False
    )
```

```python
import functools

import jax
import jax.numpy as jnp
from jax import lax
from jax.experimental import pallas as pl
from jax.experimental.pallas import tpu as pltpu
from jax.sharding import PartitionSpec as P

LANES = 128
VMEM = 62 * 1024 * 1024
FREE = pl.CostEstimate(flops=0, bytes_accessed=0, transcendentals=0)
LONG = pl.CostEstimate(flops=20 * 10**9, bytes_accessed=0, transcendentals=0)
ANY = pl.BlockSpec(memory_space=pl.ANY)
SMEM = pl.BlockSpec(memory_space=pltpu.SMEM)


def gate_table(expert_ids, gate_weights, experts):
    named = expert_ids[:, :, None] == jnp.arange(experts, dtype=jnp.int32)
    return jnp.sum(jnp.where(named, gate_weights[:, :, None], 0.0), axis=1)


def pack(table, width):
    parts, rest = [], table
    for _ in range(3):
        part = lax.reduce_precision(rest, 8, 7)
        parts.append(part.astype(jnp.bfloat16))
        rest = rest - part
    flat = jnp.concatenate(parts, axis=0).reshape(-1)
    rows = -(-flat.shape[0] // (16 * width)) * 16
    return jnp.pad(flat, (0, rows * width - flat.shape[0])).reshape(rows, width)


def unpack(packed, count, columns):
    parts = packed.reshape(-1)[: 3 * count * columns].reshape(3, count, columns).astype(jnp.float32)
    return parts[0] + parts[1] + parts[2]


def after(array, *earlier):
    return lax.optimization_barrier((array, *earlier))[0]


class Loads:
    def __init__(self, sems):
        self.sems, self.used = sems, 0

    def add(self, source, target):
        self.used += 1
        return pltpu.make_async_copy(source, target, self.sems.at[self.used - 1])


def row_loads(loads, row_refs, rows, numbers_ref, slices, depth):
    tok_rows, span = row_refs[0].shape[0], 2 * depth
    copies = []
    for j in range(slices // 2):
        columns = pl.ds(pl.multiple_of(numbers_ref[slices + j], LANES), span)
        for b, row_ref in enumerate(row_refs):
            target = rows.at[pl.ds(b * tok_rows, tok_rows), pl.ds(j * span, span)]
            copies.append(loads.add(row_ref.at[:, columns], target))
    return copies


def weight_loads(loads, weight_refs, weights, numbers_ref, tiles, tile):
    depth, both = weight_refs[0].shape
    copies = []
    for t in range(tiles):
        copies.append([])
        for k, weight_ref in enumerate(weight_refs):
            place = pl.ds(pl.multiple_of(numbers_ref[k], LANES), depth)
            for part in range(2):
                source = weight_ref.at[:, pl.ds(part * (both // 2) + t * tile, tile)]
                target = weights.at[t, place, pl.ds(part * tile, tile)]
                copies[t].append(loads.add(source, target))
    return copies


def early_kernel(blocks, slices, numbers_ref, *refs):
    row_refs, refs = refs[:blocks], refs[blocks:]
    weight_refs, (gate_out, up_out, rows, weights, sems) = refs[:slices], refs[slices:]
    tiles, _, twice = weights.shape
    tile = twice // 2
    step = pl.program_id(0)
    loads = Loads(sems)
    first = row_loads(loads, row_refs, rows, numbers_ref, slices, weight_refs[0].shape[0])
    by_tile = weight_loads(loads, weight_refs, weights, numbers_ref, tiles, tile)

    @pl.when(step == 0)
    def _():
        for copy in first + [copy for copies in by_tile for copy in copies]:
            copy.start()
        for copy in first:
            copy.wait()

    for t in range(tiles):

        @pl.when(step == t)
        def _():
            for copy in by_tile[t]:
                copy.wait()
            sums = jnp.dot(rows[...], weights[t], preferred_element_type=jnp.float32)
            gate_out[...] = sums[:, :tile]
            up_out[...] = sums[:, tile:]


def late_kernel(blocks, slices, down_slices, tile, summed, numbers_ref, *refs):
    row_refs, refs = refs[:blocks], refs[blocks:]
    weight_refs, refs = refs[:slices], refs[slices:]
    down_refs, refs = refs[:down_slices], refs[down_slices:]
    sums_in, refs = refs[:summed], refs[summed:]
    hidden, out_refs, refs = refs[0], refs[1 : 1 + blocks], refs[1 + blocks :]
    sums, (rows, weights, down, sems) = refs[:summed], refs[summed:]
    depth, both = weight_refs[0].shape
    loads = Loads(sems)
    first = row_loads(loads, row_refs, rows, numbers_ref, slices, depth)
    for k, weight_ref in enumerate(weight_refs):
        place = pl.ds(pl.multiple_of(numbers_ref[k], LANES), depth)
        first.append(loads.add(weight_ref, weights.at[place]))
    first += [loads.add(source, target) for source, target in zip(sums_in, sums)]
    final = [loads.add(ref.at[pl.ds(0, both // 2)], down.at[k]) for k, ref in enumerate(down_refs)]
    for copy in first + final:
        copy.start()
    for copy in first:
        copy.wait()
    for start in range(0, both // 2, tile):
        columns, up_columns = pl.ds(start, tile), pl.ds(both // 2 + start, tile)
        gate_sum = jnp.dot(rows[...], weights[:, columns], preferred_element_type=jnp.float32)
        up_sum = jnp.dot(rows[...], weights[:, up_columns], preferred_element_type=jnp.float32)
        if summed:
            gate_sum, up_sum = gate_sum + sums[0][:, columns], up_sum + sums[1][:, columns]
        hidden[:, columns] = (gate_sum / (1.0 + jnp.exp(-gate_sum)) * up_sum).astype(jnp.bfloat16)
    for copy in final:
        copy.wait()
    first_down = slices + slices // 2
    write_out(hidden, [down.at[k] for k in range(down_slices)], out_refs, numbers_ref, first_down)


def write_out(hidden, down, out_refs, numbers_ref, at):
    tok_rows = out_refs[0].shape[0]
    for k, weights in enumerate(down):
        part = jnp.dot(hidden[...], weights[: hidden.shape[1]], preferred_element_type=jnp.float32).astype(jnp.bfloat16)
        columns = pl.ds(pl.multiple_of(numbers_ref[at + k], LANES), part.shape[1])
        for b, out_ref in enumerate(out_refs):
            out_ref[:, columns] = part[b * tok_rows : (b + 1) * tok_rows]


def early_sums(row_blocks, gate_up, numbers):
    blocks, slices = len(row_blocks), len(gate_up)
    depth, both = gate_up[0].shape
    count, inner = blocks * row_blocks[0].shape[0], both // 2
    tile = 256 if inner % 256 == 0 else inner
    tiles = inner // tile
    spec = pl.BlockSpec((count, tile), lambda i: (0, i))
    return pl.pallas_call(
        functools.partial(early_kernel, blocks, slices),
        grid=(tiles,),
        in_specs=[SMEM] + [ANY] * (blocks + slices),
        out_specs=[spec, spec],
        out_shape=[jax.ShapeDtypeStruct((count, inner), jnp.float32)] * 2,
        scratch_shapes=[
            pltpu.VMEM((count, slices * depth), jnp.bfloat16),
            pltpu.VMEM((tiles, slices * depth, 2 * tile), jnp.bfloat16),
            pltpu.SemaphoreType.DMA((slices // 2 * blocks + 2 * tiles * slices,)),
        ],
        compiler_params=pltpu.CompilerParams(vmem_limit_bytes=62 * 1024 * 1024),
        cost_estimate=FREE,
    )(numbers, *row_blocks, *gate_up)


def late_outputs(row_blocks, gate_up, down, numbers, early):
    blocks, slices, down_slices = len(row_blocks), len(gate_up), len(down)
    depth, both = gate_up[0].shape
    tok_rows = row_blocks[0].shape[0]
    count, inner = blocks * tok_rows, both // 2
    tile = 256 if inner % 256 == 0 else inner
    whole = pl.BlockSpec(memory_space=pltpu.VMEM)
    out = jax.ShapeDtypeStruct((tok_rows, down_slices * depth), jnp.bfloat16)
    results = pl.pallas_call(
        functools.partial(late_kernel, blocks, slices, down_slices, tile, len(early)),
        in_specs=[SMEM] + [ANY] * (blocks + slices + down_slices + len(early)),
        out_specs=[whole] * (1 + blocks),
        out_shape=[jax.ShapeDtypeStruct((count, inner), jnp.bfloat16)] + [out] * blocks,
        scratch_shapes=[pltpu.VMEM((count, inner), jnp.float32)] * len(early)
        + [
            pltpu.VMEM((count, slices * depth), jnp.bfloat16),
            pltpu.VMEM((slices * depth, both), jnp.bfloat16),
            pltpu.VMEM((down_slices, inner, down[0].shape[1]), jnp.bfloat16),
            pltpu.SemaphoreType.DMA((slices // 2 * blocks + slices + 2 + down_slices,)),
        ],
        compiler_params=pltpu.CompilerParams(vmem_limit_bytes=62 * 1024 * 1024),
        cost_estimate=FREE,
    )(numbers, *row_blocks, *gate_up, *down, *early)
    return results[0], results[1:]


def down_kernel(blocks, slices, numbers_ref, hidden_ref, *refs):
    write_out(hidden_ref, refs[:slices], refs[slices:], numbers_ref, 0)


def outputs_of(hidden, blocks, down, numbers):
    count, inner = hidden.shape
    slices, depth = len(down), down[0].shape[1]
    whole = pl.BlockSpec(memory_space=pltpu.VMEM)
    return pl.pallas_call(
        functools.partial(down_kernel, blocks, slices),
        in_specs=[SMEM] + [whole] * (1 + slices),
        out_specs=[whole] * blocks,
        out_shape=[jax.ShapeDtypeStruct((count // blocks, slices * depth), jnp.bfloat16)] * blocks,
        compiler_params=pltpu.CompilerParams(vmem_limit_bytes=24 * 1024 * 1024),
        cost_estimate=FREE,
    )(numbers, hidden, *down)


def finish_kernel(mine, bases_ref, gates_ref, *refs):
    parts, sums, out_ref = refs[:mine], refs[mine:-1], refs[-1]
    for group, ref in enumerate(sums):
        columns = pl.ds(pl.multiple_of(bases_ref[group], LANES), ref.shape[1])
        total = ref[...].astype(jnp.float32)
        for k, part in enumerate(parts):
            total += part[:, columns].astype(jnp.float32) * gates_ref[:, k : k + 1]
        out_ref[:, columns] = total.astype(jnp.bfloat16)


def shards(tokens, expert_ids, gate_weights, hot_ids, w_gate, w_up, w_down):
    del hot_ids
    tok_rows, model = tokens.shape
    places, lines = lax.axis_size("expert"), lax.axis_size("dp")
    layers = lines // 2
    half = layers // 2
    mirror = layers - 1
    local_count, depth = w_gate.shape[:2]
    experts = places * local_count
    assert local_count == 2 and half % 2 == 0

    def swap_layer(array, mask):
        return lax.ppermute(array, "dp", [(i, i ^ (2 * mask)) for i in range(lines)])

    def swap_core(array):
        return lax.ppermute(array, "dp", [(i, i ^ 1) for i in range(lines)])

    def swap_place(array, mask):
        return lax.ppermute(array, "expert", [(i, i ^ mask) for i in range(places)])

    line = lax.axis_index("dp")
    layer = line // 2
    parity = lax.rem(layer, 2)
    side = line // (lines // 2)
    near, away = list(range(half)), list(range(half, layers))
    soon, last = near + [mirror], away[:-1]

    def pick(array, which):
        return lax.dynamic_index_in_dim(array, which, 0, keepdims=False)

    def numbers(values):
        return jnp.stack([jnp.asarray(v, jnp.int32) for v in values])

    def lines_of(masks):
        return [line ^ (2 * mask + core) for mask in masks for core in range(2)]

    def places_of(masks):
        first = [2 * (layer ^ mask) * depth for mask in masks]
        return numbers([(2 * (k // 2) + lax.rem(v, 2)) * depth for k, v in enumerate(lines_of(masks))] + first)

    def both_cores(found, found_core, masks):
        return [piece for mask in masks for piece in (found[mask], found_core[mask])]

    singles = [1 << i for i in range(places.bit_length() - 1)]
    others = [mask for mask in range(1, places) if mask not in singles]
    block = tokens
    dn = {0: pick(w_down, side)}
    far = {0: swap_layer(block, mirror)}
    own = {0: block, **{mask: swap_place(block, mask) for mask in range(1, places)}}
    for mask in near[1:]:
        dn[mask] = swap_layer(dn[0], mask)
    wave = [far[0], *[own[mask] for mask in singles], *[dn[mask] for mask in near[1:]]]
    first = [far[0], *[dn[mask] for mask in near[1:]]]

    table = gate_table(expert_ids, gate_weights, experts)
    carried = jnp.concatenate([pick(w_down, 1 - side), pack(table, depth)], axis=0)
    mine, theirs = [jnp.concatenate([pick(w_gate, which), pick(w_up, which)], axis=1) for which in (side, 1 - side)]
    gu = {0: mine, mirror: swap_layer(after(theirs, carried, *first), mirror)}
    for mask in near[1:]:
        gu[mask] = swap_layer(after(mine, *first), mask)
    for mask in singles:
        far[mask] = swap_place(after(far[0], *wave), mask)
    for mask in others:
        far[mask] = swap_place(after(far[0], *wave), mask)
    wave = [gu[mirror], *[gu[mask] for mask in near[1:]], *[far[mask] for mask in range(1, places)], *[own[mask] for mask in others]]


    def gates_of(table):
        place = lax.axis_index("expert")
        wanted = jnp.stack([(place ^ mask) * local_count + side for mask in range(places)])
        chosen = jnp.arange(experts, dtype=jnp.int32)[:, None] == wanted
        return jnp.sum(jnp.where(chosen, table[:, :, None], 0.0), axis=1)

    own_gates = gates_of(table)

    for mask in near[1:]:
        gu[mask ^ mirror] = swap_layer(after(gu[mirror], *wave), mask)
    dn[mirror] = swap_layer(after(carried, *wave), mirror)
    gu_core = {mask: swap_core(after(gu[mask], *wave)) for mask in near + [mirror]}
    pieces = both_cores(gu, gu_core, soon)
    chunks = {}
    for key, found in (("far", far), ("own", own)):
        blocks = [found[mask] for mask in range(places)]
        chunks[key] = [blocks[i : i + 4] for i in range(0, places, 4)]
    counted = after(places_of(soon), dn[mirror])
    early = [early_sums(chunk, pieces, counted) for chunk in chunks["far"]]
    settled = [sums for pair in early for sums in pair]
    dn_core = {mask: swap_core(after(dn[mask], dn[mirror])) for mask in near}
    wave = [*settled, *[dn_core[mask] for mask in near]]
    for mask in near[1:]:
        gu_core[mask ^ mirror] = swap_core(after(gu[mask ^ mirror], *wave))

    far_gates = gates_of(unpack(dn[mirror][w_down.shape[1] :], tok_rows, experts))

    def arrived(parts):
        return [parts[0]] + [swap_place(parts[mask], mask) for mask in range(1, places)]

    def add_up(parts, gates):
        total = parts[0].astype(jnp.float32) * gates[:, :1]
        for k, part in enumerate(parts[1:], 1):
            total += part.astype(jnp.float32) * gates[:, k : k + 1]
        return total.astype(jnp.bfloat16)

    def late(chunks, gate_masks, down_masks, early):
        columns = [lax.rem(v, 2 * len(down_masks)) * depth for v in lines_of(down_masks)]
        counted = jnp.concatenate([places_of(gate_masks), numbers(columns)])
        hidden, parts = [], []
        for chunk, sums in zip(chunks, early):
            pieces = both_cores(gu, gu_core, gate_masks)
            rows, blocks = late_outputs(chunk, pieces, both_cores(dn, dn_core, down_masks), counted, sums)
            hidden.append(rows)
            parts += blocks
        return hidden, parts

    far_hidden, far_parts = late(chunks["far"], last, near, early)
    for mask in near[1:]:
        dn[mask ^ mirror] = swap_layer(after(dn[mirror], *settled), mask)
    for mask in away:
        dn_core[mask] = swap_core(after(dn[mask], far_hidden[-1]))
    starts = numbers([lax.rem(v, 2 * len(away)) * depth for v in lines_of(away)])
    more_parts = []
    for chunk, rows in zip(chunks["far"], far_hidden):
        more_parts += outputs_of(rows, len(chunk), both_cores(dn, dn_core, away), starts)
    arrived_near = arrived(far_parts)
    near_total = add_up(arrived_near, far_gates)
    arrived_away = arrived(more_parts)
    away_total = add_up([after(part, near_total, *arrived_near) for part in arrived_away], far_gates)
    sums = [swap_layer(total, mirror) for total in (near_total, away_total)]
    mine = arrived(late(chunks["own"], soon + last, near + away, [()] * len(chunks["own"]))[1])
    width = model // 2
    bases = numbers([(1 - side) * width, side * width])
    whole = pl.BlockSpec(memory_space=pltpu.VMEM)
    return pl.pallas_call(
        functools.partial(finish_kernel, len(mine)),
        in_specs=[SMEM] + [whole] * (1 + len(mine) + len(sums)),
        out_specs=whole,
        out_shape=jax.ShapeDtypeStruct((tok_rows, model), jnp.bfloat16),
        compiler_params=pltpu.CompilerParams(vmem_limit_bytes=16 * 1024 * 1024),
    )(bases, own_gates, *mine, *sums)


def solution(mesh):
    placed = (
        P(("dp", "expert"), None),
        P(("dp", "expert"), None),
        P(("dp", "expert"), None),
        P(),
        P("expert", "dp", None),
        P("expert", "dp", None),
        P("expert", None, "dp"),
    )
    return jax.shard_map(
        shards, mesh=mesh, in_specs=placed, out_specs=P(("dp", "expert"), None), check_vma=False
    )
```

```python
import functools

import jax
import jax.numpy as jnp
from jax import lax
from jax.experimental import pallas as pl
from jax.experimental.pallas import tpu as pltpu
from jax.sharding import PartitionSpec as P

LANES = 128
VMEM = 62 * 1024 * 1024
FREE = pl.CostEstimate(flops=0, bytes_accessed=0, transcendentals=0)
LONG = pl.CostEstimate(flops=20 * 10**9, bytes_accessed=0, transcendentals=0)
ANY = pl.BlockSpec(memory_space=pl.ANY)
SMEM = pl.BlockSpec(memory_space=pltpu.SMEM)


def gate_table(expert_ids, gate_weights, experts):
    named = expert_ids[:, :, None] == jnp.arange(experts, dtype=jnp.int32)
    return jnp.sum(jnp.where(named, gate_weights[:, :, None], 0.0), axis=1)


def pack(table, width):
    parts, rest = [], table
    for _ in range(3):
        part = lax.reduce_precision(rest, 8, 7)
        parts.append(part.astype(jnp.bfloat16))
        rest = rest - part
    flat = jnp.concatenate(parts, axis=0).reshape(-1)
    rows = -(-flat.shape[0] // (16 * width)) * 16
    return jnp.pad(flat, (0, rows * width - flat.shape[0])).reshape(rows, width)


def unpack(packed, count, columns):
    parts = packed.reshape(-1)[: 3 * count * columns].reshape(3, count, columns).astype(jnp.float32)
    return parts[0] + parts[1] + parts[2]


def after(array, *earlier):
    return lax.optimization_barrier((array, *earlier))[0]


class Loads:
    def __init__(self, sems):
        self.sems, self.used = sems, 0

    def add(self, source, target):
        self.used += 1
        return pltpu.make_async_copy(source, target, self.sems.at[self.used - 1])


def row_loads(loads, row_refs, rows, numbers_ref, slices, depth):
    tok_rows, span = row_refs[0].shape[0], 2 * depth
    copies = []
    for j in range(slices // 2):
        columns = pl.ds(pl.multiple_of(numbers_ref[slices + j], LANES), span)
        for b, row_ref in enumerate(row_refs):
            target = rows.at[pl.ds(b * tok_rows, tok_rows), pl.ds(j * span, span)]
            copies.append(loads.add(row_ref.at[:, columns], target))
    return copies


def weight_loads(loads, weight_refs, weights, numbers_ref, tiles, tile):
    depth, both = weight_refs[0].shape
    copies = []
    for t in range(tiles):
        copies.append([])
        for k, weight_ref in enumerate(weight_refs):
            place = pl.ds(pl.multiple_of(numbers_ref[k], LANES), depth)
            for part in range(2):
                source = weight_ref.at[:, pl.ds(part * (both // 2) + t * tile, tile)]
                target = weights.at[t, place, pl.ds(part * tile, tile)]
                copies[t].append(loads.add(source, target))
    return copies


def early_kernel(blocks, slices, numbers_ref, *refs):
    row_refs, refs = refs[:blocks], refs[blocks:]
    weight_refs, (gate_out, up_out, rows, weights, sems) = refs[:slices], refs[slices:]
    tiles, _, twice = weights.shape
    tile = twice // 2
    step = pl.program_id(0)
    loads = Loads(sems)
    first = row_loads(loads, row_refs, rows, numbers_ref, slices, weight_refs[0].shape[0])
    by_tile = weight_loads(loads, weight_refs, weights, numbers_ref, tiles, tile)

    @pl.when(step == 0)
    def _():
        for copy in first + [copy for copies in by_tile for copy in copies]:
            copy.start()
        for copy in first:
            copy.wait()

    for t in range(tiles):

        @pl.when(step == t)
        def _():
            for copy in by_tile[t]:
                copy.wait()
            sums = jnp.dot(rows[...], weights[t], preferred_element_type=jnp.float32)
            gate_out[...] = sums[:, :tile]
            up_out[...] = sums[:, tile:]


def late_kernel(blocks, pieces, down_slices, tile, summed, numbers_ref, *refs):
    row_refs, refs = refs[:blocks], refs[blocks:]
    slices = len(pieces)
    weight_refs, refs = refs[: sum(pieces)], refs[sum(pieces) :]
    down_refs, refs = refs[:down_slices], refs[down_slices:]
    sums_in, refs = refs[:summed], refs[summed:]
    hidden, out_refs, refs = refs[0], refs[1 : 1 + blocks], refs[1 + blocks :]
    sums, (rows, weights, down, sems) = refs[:summed], refs[summed:]
    depth, both = weight_refs[0].shape[0], weights.shape[1]
    loads = Loads(sems)
    first = row_loads(loads, row_refs, rows, numbers_ref, slices, depth)
    left = list(weight_refs)
    for k, number in enumerate(pieces):
        place, width = pl.ds(pl.multiple_of(numbers_ref[k], LANES), depth), both // number
        for part in range(number):
            first.append(loads.add(left.pop(0), weights.at[place, pl.ds(part * width, width)]))
    first += [loads.add(source, target) for source, target in zip(sums_in, sums)]
    final = [loads.add(ref.at[pl.ds(0, both // 2)], down.at[k]) for k, ref in enumerate(down_refs)]
    for copy in first + final:
        copy.start()
    for copy in first:
        copy.wait()
    for start in range(0, both // 2, tile):
        columns, up_columns = pl.ds(start, tile), pl.ds(both // 2 + start, tile)
        gate_sum = jnp.dot(rows[...], weights[:, columns], preferred_element_type=jnp.float32)
        up_sum = jnp.dot(rows[...], weights[:, up_columns], preferred_element_type=jnp.float32)
        if summed:
            gate_sum, up_sum = gate_sum + sums[0][:, columns], up_sum + sums[1][:, columns]
        hidden[:, columns] = (gate_sum / (1.0 + jnp.exp(-gate_sum)) * up_sum).astype(jnp.bfloat16)
    for copy in final:
        copy.wait()
    first_down = slices + slices // 2
    write_out(hidden, [down.at[k] for k in range(down_slices)], out_refs, numbers_ref, first_down)


def write_out(hidden, down, out_refs, numbers_ref, at):
    tok_rows = out_refs[0].shape[0]
    for k, weights in enumerate(down):
        part = jnp.dot(hidden[...], weights[: hidden.shape[1]], preferred_element_type=jnp.float32).astype(jnp.bfloat16)
        columns = pl.ds(pl.multiple_of(numbers_ref[at + k], LANES), part.shape[1])
        for b, out_ref in enumerate(out_refs):
            out_ref[:, columns] = part[b * tok_rows : (b + 1) * tok_rows]


def early_sums(row_blocks, gate_up, numbers):
    blocks, slices = len(row_blocks), len(gate_up)
    depth, both = gate_up[0].shape
    count, inner = blocks * row_blocks[0].shape[0], both // 2
    tile = 256 if inner % 256 == 0 else inner
    tiles = inner // tile
    spec = pl.BlockSpec((count, tile), lambda i: (0, i))
    return pl.pallas_call(
        functools.partial(early_kernel, blocks, slices),
        grid=(tiles,),
        in_specs=[SMEM] + [ANY] * (blocks + slices),
        out_specs=[spec, spec],
        out_shape=[jax.ShapeDtypeStruct((count, inner), jnp.float32)] * 2,
        scratch_shapes=[
            pltpu.VMEM((count, slices * depth), jnp.bfloat16),
            pltpu.VMEM((tiles, slices * depth, 2 * tile), jnp.bfloat16),
            pltpu.SemaphoreType.DMA((slices // 2 * blocks + 2 * tiles * slices,)),
        ],
        compiler_params=pltpu.CompilerParams(vmem_limit_bytes=62 * 1024 * 1024),
        cost_estimate=FREE,
    )(numbers, *row_blocks, *gate_up)


def late_outputs(row_blocks, gate_up, down, numbers, early):
    blocks, slices, down_slices = len(row_blocks), len(gate_up), len(down)
    depth, both = gate_up[0][0].shape[0], sum(piece.shape[1] for piece in gate_up[0])
    pieces = tuple(len(parts) for parts in gate_up)
    gate_up = [piece for parts in gate_up for piece in parts]
    tok_rows = row_blocks[0].shape[0]
    count, inner = blocks * tok_rows, both // 2
    tile = 256 if inner % 256 == 0 else inner
    whole = pl.BlockSpec(memory_space=pltpu.VMEM)
    out = jax.ShapeDtypeStruct((tok_rows, down_slices * depth), jnp.bfloat16)
    results = pl.pallas_call(
        functools.partial(late_kernel, blocks, pieces, down_slices, tile, len(early)),
        in_specs=[SMEM] + [ANY] * (blocks + len(gate_up) + down_slices + len(early)),
        out_specs=[whole] * (1 + blocks),
        out_shape=[jax.ShapeDtypeStruct((count, inner), jnp.bfloat16)] + [out] * blocks,
        scratch_shapes=[pltpu.VMEM((count, inner), jnp.float32)] * len(early)
        + [
            pltpu.VMEM((count, slices * depth), jnp.bfloat16),
            pltpu.VMEM((slices * depth, both), jnp.bfloat16),
            pltpu.VMEM((down_slices, inner, down[0].shape[1]), jnp.bfloat16),
            pltpu.SemaphoreType.DMA((slices // 2 * blocks + len(gate_up) + 2 + down_slices,)),
        ],
        compiler_params=pltpu.CompilerParams(vmem_limit_bytes=62 * 1024 * 1024),
        cost_estimate=FREE,
    )(numbers, *row_blocks, *gate_up, *down, *early)
    return results[0], results[1:]


def down_kernel(blocks, slices, numbers_ref, hidden_ref, *refs):
    write_out(hidden_ref, refs[:slices], refs[slices:], numbers_ref, 0)


def outputs_of(hidden, blocks, down, numbers):
    count, inner = hidden.shape
    slices, depth = len(down), down[0].shape[1]
    whole = pl.BlockSpec(memory_space=pltpu.VMEM)
    return pl.pallas_call(
        functools.partial(down_kernel, blocks, slices),
        in_specs=[SMEM] + [whole] * (1 + slices),
        out_specs=[whole] * blocks,
        out_shape=[jax.ShapeDtypeStruct((count // blocks, slices * depth), jnp.bfloat16)] * blocks,
        compiler_params=pltpu.CompilerParams(vmem_limit_bytes=24 * 1024 * 1024),
        cost_estimate=FREE,
    )(numbers, hidden, *down)


def finish_kernel(mine, bases_ref, gates_ref, *refs):
    parts, sums, out_ref = refs[:mine], refs[mine:-1], refs[-1]
    for group, ref in enumerate(sums):
        columns = pl.ds(pl.multiple_of(bases_ref[group], LANES), ref.shape[1])
        total = ref[...].astype(jnp.float32)
        for k, part in enumerate(parts):
            total += part[:, columns].astype(jnp.float32) * gates_ref[:, k : k + 1]
        out_ref[:, columns] = total.astype(jnp.bfloat16)


def shards(tokens, expert_ids, gate_weights, hot_ids, w_gate, w_up, w_down):
    del hot_ids
    tok_rows, model = tokens.shape
    places, lines = lax.axis_size("expert"), lax.axis_size("dp")
    layers = lines // 2
    half = layers // 2
    mirror = layers - 1
    local_count, depth = w_gate.shape[:2]
    experts = places * local_count
    assert local_count == 2 and half % 2 == 0

    def swap_layer(array, mask):
        return lax.ppermute(array, "dp", [(i, i ^ (2 * mask)) for i in range(lines)])

    def swap_core(array):
        return lax.ppermute(array, "dp", [(i, i ^ 1) for i in range(lines)])

    def swap_place(array, mask):
        return lax.ppermute(array, "expert", [(i, i ^ mask) for i in range(places)])

    line = lax.axis_index("dp")
    layer = line // 2
    parity = lax.rem(layer, 2)
    side = line // (lines // 2)
    near, away = list(range(half)), list(range(half, layers))
    soon, last = near + [mirror], away[:-1]

    def pick(array, which):
        return lax.dynamic_index_in_dim(array, which, 0, keepdims=False)

    def numbers(values):
        return jnp.stack([jnp.asarray(v, jnp.int32) for v in values])

    def lines_of(masks):
        return [line ^ (2 * mask + core) for mask in masks for core in range(2)]

    def places_of(masks):
        first = [2 * (layer ^ mask) * depth for mask in masks]
        return numbers([(2 * (k // 2) + lax.rem(v, 2)) * depth for k, v in enumerate(lines_of(masks))] + first)

    def both_cores(found, found_core, masks):
        return [piece for mask in masks for piece in (found[mask], found_core[mask])]

    singles = [1 << i for i in range(places.bit_length() - 1)]
    others = [mask for mask in range(1, places) if mask not in singles]
    block = tokens
    dn = {0: pick(w_down, side)}
    far = {0: swap_layer(block, mirror)}
    own = {0: block, **{mask: swap_place(block, mask) for mask in range(1, places)}}
    for mask in near[1:]:
        dn[mask] = swap_layer(dn[0], mask)
    wave = [far[0], *[own[mask] for mask in singles], *[dn[mask] for mask in near[1:]]]
    first = [far[0], *[dn[mask] for mask in near[1:]]]

    table = gate_table(expert_ids, gate_weights, experts)
    carried = jnp.concatenate([pick(w_down, 1 - side), pack(table, depth)], axis=0)
    mine, theirs = [jnp.concatenate([pick(w_gate, which), pick(w_up, which)], axis=1) for which in (side, 1 - side)]
    gu = {0: mine, mirror: swap_layer(after(theirs, carried, *first), mirror)}
    for mask in near[1:]:
        gu[mask] = swap_layer(after(mine, *first), mask)
    for mask in singles:
        far[mask] = swap_place(after(far[0], *wave), mask)
    for mask in others:
        far[mask] = swap_place(after(far[0], *wave), mask)
    wave = [gu[mirror], *[gu[mask] for mask in near[1:]], *[far[mask] for mask in range(1, places)], *[own[mask] for mask in others]]


    def gates_of(table):
        place = lax.axis_index("expert")
        wanted = jnp.stack([(place ^ mask) * local_count + side for mask in range(places)])
        chosen = jnp.arange(experts, dtype=jnp.int32)[:, None] == wanted
        return jnp.sum(jnp.where(chosen, table[:, :, None], 0.0), axis=1)

    own_gates = gates_of(table)

    for mask in near[1:]:
        gu[mask ^ mirror] = swap_layer(after(gu[mirror], *wave), mask)
    dn[mirror] = swap_layer(after(carried, *wave), mirror)
    gu_core = {mask: swap_core(after(gu[mask], *wave)) for mask in near + [mirror]}
    pieces = both_cores(gu, gu_core, soon)
    chunks = {}
    for key, found in (("far", far), ("own", own)):
        blocks = [found[mask] for mask in range(places)]
        chunks[key] = [blocks[i : i + 4] for i in range(0, places, 4)]
    counted = after(places_of(soon), dn[mirror])
    early = [early_sums(chunk, pieces, counted) for chunk in chunks["far"]]
    settled = [sums for pair in early for sums in pair]
    dn_core = {mask: swap_core(after(dn[mask], dn[mirror])) for mask in near}
    wave = [*settled, *[dn_core[mask] for mask in near]]
    for mask in near[1:]:
        held = after(gu[mask ^ mirror], *wave)
        parts = (held[:, : held.shape[1] // 2], held[:, held.shape[1] // 2 :])
        gu_core[mask ^ mirror] = [swap_core(part) for part in parts]

    far_gates = gates_of(unpack(dn[mirror][w_down.shape[1] :], tok_rows, experts))

    def arrived(parts):
        return [parts[0]] + [swap_place(parts[mask], mask) for mask in range(1, places)]

    def add_up(parts, gates):
        total = parts[0].astype(jnp.float32) * gates[:, :1]
        for k, part in enumerate(parts[1:], 1):
            total += part.astype(jnp.float32) * gates[:, k : k + 1]
        return total.astype(jnp.bfloat16)

    def late(chunks, gate_masks, down_masks, early):
        columns = [lax.rem(v, 2 * len(down_masks)) * depth for v in lines_of(down_masks)]
        counted = jnp.concatenate([places_of(gate_masks), numbers(columns)])
        hidden, parts = [], []
        for chunk, sums in zip(chunks, early):
            pieces = [found if isinstance(found, list) else [found] for found in both_cores(gu, gu_core, gate_masks)]
            rows, blocks = late_outputs(chunk, pieces, both_cores(dn, dn_core, down_masks), counted, sums)
            hidden.append(rows)
            parts += blocks
        return hidden, parts

    far_hidden, far_parts = late(chunks["far"], last, near, early)
    for mask in near[1:]:
        dn[mask ^ mirror] = swap_layer(after(dn[mirror], *settled), mask)
    for mask in away:
        dn_core[mask] = swap_core(after(dn[mask], far_hidden[-1]))
    starts = numbers([lax.rem(v, 2 * len(away)) * depth for v in lines_of(away)])
    more_parts = []
    for chunk, rows in zip(chunks["far"], far_hidden):
        more_parts += outputs_of(rows, len(chunk), both_cores(dn, dn_core, away), starts)
    arrived_near = arrived(far_parts)
    near_total = add_up(arrived_near, far_gates)
    arrived_away = arrived(more_parts)
    away_total = add_up([after(part, near_total, *arrived_near) for part in arrived_away], far_gates)
    sums = [swap_layer(total, mirror) for total in (near_total, away_total)]
    mine = arrived(late(chunks["own"], soon + last, near + away, [()] * len(chunks["own"]))[1])
    width = model // 2
    bases = numbers([(1 - side) * width, side * width])
    whole = pl.BlockSpec(memory_space=pltpu.VMEM)
    return pl.pallas_call(
        functools.partial(finish_kernel, len(mine)),
        in_specs=[SMEM] + [whole] * (1 + len(mine) + len(sums)),
        out_specs=whole,
        out_shape=jax.ShapeDtypeStruct((tok_rows, model), jnp.bfloat16),
        compiler_params=pltpu.CompilerParams(vmem_limit_bytes=16 * 1024 * 1024),
    )(bases, own_gates, *mine, *sums)


def solution(mesh):
    placed = (
        P(("dp", "expert"), None),
        P(("dp", "expert"), None),
        P(("dp", "expert"), None),
        P(),
        P("expert", "dp", None),
        P("expert", "dp", None),
        P("expert", None, "dp"),
    )
    return jax.shard_map(
        shards, mesh=mesh, in_specs=placed, out_specs=P(("dp", "expert"), None), check_vma=False
    )
```

```python
import functools

import jax
import jax.numpy as jnp
from jax import lax
from jax.experimental import pallas as pl
from jax.experimental.pallas import tpu as pltpu
from jax.sharding import PartitionSpec as P

LANES = 128
VMEM = 62 * 1024 * 1024
FREE = pl.CostEstimate(flops=0, bytes_accessed=0, transcendentals=0)
LONG = pl.CostEstimate(flops=20 * 10**9, bytes_accessed=0, transcendentals=0)
ANY = pl.BlockSpec(memory_space=pl.ANY)
SMEM = pl.BlockSpec(memory_space=pltpu.SMEM)


def gate_table(expert_ids, gate_weights, experts):
    named = expert_ids[:, :, None] == jnp.arange(experts, dtype=jnp.int32)
    return jnp.sum(jnp.where(named, gate_weights[:, :, None], 0.0), axis=1)


def pack(table, width):
    parts, rest = [], table
    for _ in range(3):
        part = lax.reduce_precision(rest, 8, 7)
        parts.append(part.astype(jnp.bfloat16))
        rest = rest - part
    flat = jnp.concatenate(parts, axis=0).reshape(-1)
    rows = -(-flat.shape[0] // (16 * width)) * 16
    return jnp.pad(flat, (0, rows * width - flat.shape[0])).reshape(rows, width)


def unpack(packed, count, columns):
    parts = packed.reshape(-1)[: 3 * count * columns].reshape(3, count, columns).astype(jnp.float32)
    return parts[0] + parts[1] + parts[2]


def after(array, *earlier):
    return lax.optimization_barrier((array, *earlier))[0]


class Loads:
    def __init__(self, sems):
        self.sems, self.used = sems, 0

    def add(self, source, target):
        self.used += 1
        return pltpu.make_async_copy(source, target, self.sems.at[self.used - 1])


def row_loads(loads, row_refs, rows, numbers_ref, slices, depth):
    tok_rows, span = row_refs[0].shape[0], 2 * depth
    copies = []
    for j in range(slices // 2):
        columns = pl.ds(pl.multiple_of(numbers_ref[slices + j], LANES), span)
        for b, row_ref in enumerate(row_refs):
            target = rows.at[pl.ds(b * tok_rows, tok_rows), pl.ds(j * span, span)]
            copies.append(loads.add(row_ref.at[:, columns], target))
    return copies


def weight_loads(loads, weight_refs, weights, numbers_ref, tiles, tile):
    depth, both = weight_refs[0].shape
    copies = []
    for t in range(tiles):
        copies.append([])
        for k, weight_ref in enumerate(weight_refs):
            place = pl.ds(pl.multiple_of(numbers_ref[k], LANES), depth)
            for part in range(2):
                source = weight_ref.at[:, pl.ds(part * (both // 2) + t * tile, tile)]
                target = weights.at[t, place, pl.ds(part * tile, tile)]
                copies[t].append(loads.add(source, target))
    return copies


def early_kernel(blocks, slices, numbers_ref, *refs):
    row_refs, refs = refs[:blocks], refs[blocks:]
    weight_refs, (gate_out, up_out, rows, weights, sems) = refs[:slices], refs[slices:]
    tiles, _, twice = weights.shape
    tile = twice // 2
    step = pl.program_id(0)
    loads = Loads(sems)
    first = row_loads(loads, row_refs, rows, numbers_ref, slices, weight_refs[0].shape[0])
    by_tile = weight_loads(loads, weight_refs, weights, numbers_ref, tiles, tile)

    @pl.when(step == 0)
    def _():
        for copy in first + [copy for copies in by_tile for copy in copies]:
            copy.start()
        for copy in first:
            copy.wait()

    for t in range(tiles):

        @pl.when(step == t)
        def _():
            for copy in by_tile[t]:
                copy.wait()
            sums = jnp.dot(rows[...], weights[t], preferred_element_type=jnp.float32)
            gate_out[...] = sums[:, :tile]
            up_out[...] = sums[:, tile:]


def late_kernel(blocks, pieces, down_slices, tile, summed, numbers_ref, *refs):
    row_refs, refs = refs[:blocks], refs[blocks:]
    slices = len(pieces)
    weight_refs, refs = refs[: sum(pieces)], refs[sum(pieces) :]
    down_refs, refs = refs[:down_slices], refs[down_slices:]
    sums_in, refs = refs[:summed], refs[summed:]
    if summed:
        hidden, out_refs, refs = refs[0], refs[1 : 1 + blocks], refs[1 + blocks :]
    else:
        hidden, out_refs, refs = refs[blocks], refs[:blocks], refs[blocks + 1 :]
    sums, (rows, weights, down, sems) = refs[:summed], refs[summed:]
    depth, both = weight_refs[0].shape[0], weights.shape[1]
    loads = Loads(sems)
    first = row_loads(loads, row_refs, rows, numbers_ref, slices, depth)
    left = list(weight_refs)
    for k, number in enumerate(pieces):
        place, width = pl.ds(pl.multiple_of(numbers_ref[k], LANES), depth), both // number
        for part in range(number):
            first.append(loads.add(left.pop(0), weights.at[place, pl.ds(part * width, width)]))
    first += [loads.add(source, target) for source, target in zip(sums_in, sums)]
    final = [loads.add(ref.at[pl.ds(0, both // 2)], down.at[k]) for k, ref in enumerate(down_refs)]
    for copy in first + final:
        copy.start()
    for copy in first:
        copy.wait()
    for start in range(0, both // 2, tile):
        columns, up_columns = pl.ds(start, tile), pl.ds(both // 2 + start, tile)
        gate_sum = jnp.dot(rows[...], weights[:, columns], preferred_element_type=jnp.float32)
        up_sum = jnp.dot(rows[...], weights[:, up_columns], preferred_element_type=jnp.float32)
        if summed:
            gate_sum, up_sum = gate_sum + sums[0][:, columns], up_sum + sums[1][:, columns]
        hidden[:, columns] = (gate_sum / (1.0 + jnp.exp(-gate_sum)) * up_sum).astype(jnp.bfloat16)
    for copy in final:
        copy.wait()
    first_down = slices + slices // 2
    write_out(hidden, [down.at[k] for k in range(down_slices)], out_refs, numbers_ref, first_down)


def write_out(hidden, down, out_refs, numbers_ref, at):
    tok_rows = out_refs[0].shape[0]
    for k, weights in enumerate(down):
        part = jnp.dot(hidden[...], weights[: hidden.shape[1]], preferred_element_type=jnp.float32).astype(jnp.bfloat16)
        columns = pl.ds(pl.multiple_of(numbers_ref[at + k], LANES), part.shape[1])
        for b, out_ref in enumerate(out_refs):
            out_ref[:, columns] = part[b * tok_rows : (b + 1) * tok_rows]


def early_sums(row_blocks, gate_up, numbers):
    blocks, slices = len(row_blocks), len(gate_up)
    depth, both = gate_up[0].shape
    count, inner = blocks * row_blocks[0].shape[0], both // 2
    tile = 256 if inner % 256 == 0 else inner
    tiles = inner // tile
    spec = pl.BlockSpec((count, tile), lambda i: (0, i))
    return pl.pallas_call(
        functools.partial(early_kernel, blocks, slices),
        grid=(tiles,),
        in_specs=[SMEM] + [ANY] * (blocks + slices),
        out_specs=[spec, spec],
        out_shape=[jax.ShapeDtypeStruct((count, inner), jnp.float32)] * 2,
        scratch_shapes=[
            pltpu.VMEM((count, slices * depth), jnp.bfloat16),
            pltpu.VMEM((tiles, slices * depth, 2 * tile), jnp.bfloat16),
            pltpu.SemaphoreType.DMA((slices // 2 * blocks + 2 * tiles * slices,)),
        ],
        compiler_params=pltpu.CompilerParams(vmem_limit_bytes=62 * 1024 * 1024),
        cost_estimate=FREE,
    )(numbers, *row_blocks, *gate_up)


def late_outputs(row_blocks, gate_up, down, numbers, early):
    blocks, slices, down_slices = len(row_blocks), len(gate_up), len(down)
    depth, both = gate_up[0][0].shape[0], sum(piece.shape[1] for piece in gate_up[0])
    pieces = tuple(len(parts) for parts in gate_up)
    gate_up = [piece for parts in gate_up for piece in parts]
    tok_rows = row_blocks[0].shape[0]
    count, inner = blocks * tok_rows, both // 2
    tile = 256 if inner % 256 == 0 else inner
    whole = pl.BlockSpec(memory_space=pltpu.VMEM)
    out = jax.ShapeDtypeStruct((tok_rows, down_slices * depth), jnp.bfloat16)
    kept = [jax.ShapeDtypeStruct((count, inner), jnp.bfloat16)] if early else []
    results = pl.pallas_call(
        functools.partial(late_kernel, blocks, pieces, down_slices, tile, len(early)),
        in_specs=[SMEM] + [ANY] * (blocks + len(gate_up) + down_slices + len(early)),
        out_specs=[whole] * (len(kept) + blocks),
        out_shape=kept + [out] * blocks,
        scratch_shapes=([pltpu.VMEM((count, inner), jnp.float32)] * len(early) or [pltpu.VMEM((count, inner), jnp.bfloat16)])
        + [
            pltpu.VMEM((count, slices * depth), jnp.bfloat16),
            pltpu.VMEM((slices * depth, both), jnp.bfloat16),
            pltpu.VMEM((down_slices, inner, down[0].shape[1]), jnp.bfloat16),
            pltpu.SemaphoreType.DMA((slices // 2 * blocks + len(gate_up) + 2 + down_slices,)),
        ],
        compiler_params=pltpu.CompilerParams(vmem_limit_bytes=62 * 1024 * 1024),
        cost_estimate=FREE,
    )(numbers, *row_blocks, *gate_up, *down, *early)
    return results[: len(kept)], results[len(kept) :]


def down_kernel(blocks, slices, numbers_ref, hidden_ref, *refs):
    write_out(hidden_ref, refs[:slices], refs[slices:], numbers_ref, 0)


def outputs_of(hidden, blocks, down, numbers):
    count, inner = hidden.shape
    slices, depth = len(down), down[0].shape[1]
    whole = pl.BlockSpec(memory_space=pltpu.VMEM)
    return pl.pallas_call(
        functools.partial(down_kernel, blocks, slices),
        in_specs=[SMEM] + [whole] * (1 + slices),
        out_specs=[whole] * blocks,
        out_shape=[jax.ShapeDtypeStruct((count // blocks, slices * depth), jnp.bfloat16)] * blocks,
        compiler_params=pltpu.CompilerParams(vmem_limit_bytes=24 * 1024 * 1024),
        cost_estimate=FREE,
    )(numbers, hidden, *down)


def finish_kernel(mine, bases_ref, gates_ref, *refs):
    parts, sums, out_ref = refs[:mine], refs[mine:-1], refs[-1]
    for group, ref in enumerate(sums):
        columns = pl.ds(pl.multiple_of(bases_ref[group], LANES), ref.shape[1])
        total = ref[...].astype(jnp.float32)
        for k, part in enumerate(parts):
            total += part[:, columns].astype(jnp.float32) * gates_ref[:, k : k + 1]
        out_ref[:, columns] = total.astype(jnp.bfloat16)


def shards(tokens, expert_ids, gate_weights, hot_ids, w_gate, w_up, w_down):
    del hot_ids
    tok_rows, model = tokens.shape
    places, lines = lax.axis_size("expert"), lax.axis_size("dp")
    layers = lines // 2
    half = layers // 2
    mirror = layers - 1
    local_count, depth = w_gate.shape[:2]
    experts = places * local_count
    assert local_count == 2 and half % 2 == 0

    def swap_layer(array, mask):
        return lax.ppermute(array, "dp", [(i, i ^ (2 * mask)) for i in range(lines)])

    def swap_core(array):
        return lax.ppermute(array, "dp", [(i, i ^ 1) for i in range(lines)])

    def swap_place(array, mask):
        return lax.ppermute(array, "expert", [(i, i ^ mask) for i in range(places)])

    line = lax.axis_index("dp")
    layer = line // 2
    parity = lax.rem(layer, 2)
    side = line // (lines // 2)
    near, away = list(range(half)), list(range(half, layers))
    soon, last = near + [mirror], away[:-1]

    def pick(array, which):
        return lax.dynamic_index_in_dim(array, which, 0, keepdims=False)

    def numbers(values):
        return jnp.stack([jnp.asarray(v, jnp.int32) for v in values])

    def lines_of(masks):
        return [line ^ (2 * mask + core) for mask in masks for core in range(2)]

    def places_of(masks):
        first = [2 * (layer ^ mask) * depth for mask in masks]
        return numbers([(2 * (k // 2) + lax.rem(v, 2)) * depth for k, v in enumerate(lines_of(masks))] + first)

    def both_cores(found, found_core, masks):
        return [piece for mask in masks for piece in (found[mask], found_core[mask])]

    singles = [1 << i for i in range(places.bit_length() - 1)]
    others = [mask for mask in range(1, places) if mask not in singles]
    block = tokens
    dn = {0: pick(w_down, side)}
    far = {0: swap_layer(block, mirror)}
    own = {0: block, **{mask: swap_place(block, mask) for mask in range(1, places)}}
    for mask in near[1:]:
        dn[mask] = swap_layer(dn[0], mask)
    wave = [far[0], *[own[mask] for mask in singles], *[dn[mask] for mask in near[1:]]]
    first = [far[0], *[dn[mask] for mask in near[1:]]]

    table = gate_table(expert_ids, gate_weights, experts)
    carried = jnp.concatenate([pick(w_down, 1 - side), pack(table, depth)], axis=0)
    mine, theirs = [jnp.concatenate([pick(w_gate, which), pick(w_up, which)], axis=1) for which in (side, 1 - side)]
    gu = {0: mine, mirror: swap_layer(after(theirs, carried, *first), mirror)}
    for mask in near[1:]:
        gu[mask] = swap_layer(after(mine, *first), mask)
    for mask in singles:
        far[mask] = swap_place(after(far[0], *wave), mask)
    for mask in others:
        far[mask] = swap_place(after(far[0], *wave), mask)
    wave = [gu[mirror], *[gu[mask] for mask in near[1:]], *[far[mask] for mask in range(1, places)], *[own[mask] for mask in others]]


    def gates_of(table):
        place = lax.axis_index("expert")
        wanted = jnp.stack([(place ^ mask) * local_count + side for mask in range(places)])
        chosen = jnp.arange(experts, dtype=jnp.int32)[:, None] == wanted
        return jnp.sum(jnp.where(chosen, table[:, :, None], 0.0), axis=1)

    own_gates = gates_of(table)

    for mask in near[1:]:
        gu[mask ^ mirror] = swap_layer(after(gu[mirror], *wave), mask)
    dn[mirror] = swap_layer(after(carried, *wave), mirror)
    gu_core = {mask: swap_core(after(gu[mask], *wave)) for mask in near + [mirror]}
    pieces = both_cores(gu, gu_core, soon)
    chunks = {}
    for key, found in (("far", far), ("own", own)):
        blocks = [found[mask] for mask in range(places)]
        chunks[key] = [blocks[i : i + 4] for i in range(0, places, 4)]
    counted = after(places_of(soon), dn[mirror])
    early = [early_sums(chunk, pieces, counted) for chunk in chunks["far"]]
    settled = [sums for pair in early for sums in pair]
    dn_core = {mask: swap_core(after(dn[mask], dn[mirror])) for mask in near}
    wave = [*settled, *[dn_core[mask] for mask in near]]
    for mask in near[1:]:
        held = after(gu[mask ^ mirror], *wave)
        parts = (held[:, : held.shape[1] // 2], held[:, held.shape[1] // 2 :])
        gu_core[mask ^ mirror] = [swap_core(part) for part in parts]

    far_gates = gates_of(unpack(dn[mirror][w_down.shape[1] :], tok_rows, experts))

    def arrived(parts):
        return [parts[0]] + [swap_place(parts[mask], mask) for mask in range(1, places)]

    def add_up(parts, gates):
        total = parts[0].astype(jnp.float32) * gates[:, :1]
        for k, part in enumerate(parts[1:], 1):
            total += part.astype(jnp.float32) * gates[:, k : k + 1]
        return total.astype(jnp.bfloat16)

    def late(chunks, gate_masks, down_masks, early):
        columns = [lax.rem(v, 2 * len(down_masks)) * depth for v in lines_of(down_masks)]
        counted = jnp.concatenate([places_of(gate_masks), numbers(columns)])
        hidden, parts = [], []
        for chunk, sums in zip(chunks, early):
            pieces = [found if isinstance(found, list) else [found] for found in both_cores(gu, gu_core, gate_masks)]
            rows, blocks = late_outputs(chunk, pieces, both_cores(dn, dn_core, down_masks), counted, sums)
            hidden += rows
            parts += blocks
        return hidden, parts

    far_hidden, far_parts = late(chunks["far"], last, near, early)
    for mask in near[1:]:
        dn[mask ^ mirror] = swap_layer(after(dn[mirror], *settled), mask)
    for mask in away:
        dn_core[mask] = swap_core(after(dn[mask], *((far_hidden[-1],) if mask != mirror else settled)))
    starts = numbers([lax.rem(v, 2 * len(away)) * depth for v in lines_of(away)])
    more_parts = []
    for chunk, rows in zip(chunks["far"], far_hidden):
        more_parts += outputs_of(rows, len(chunk), both_cores(dn, dn_core, away), starts)
    arrived_near = arrived(far_parts)
    near_total = add_up(arrived_near, far_gates)
    arrived_away = arrived(more_parts)
    away_total = add_up([after(part, near_total, *arrived_near) for part in arrived_away], far_gates)
    sums = [swap_layer(total, mirror) for total in (near_total, away_total)]
    mine = arrived(late(chunks["own"], soon + last, near + away, [()] * len(chunks["own"]))[1])
    width = model // 2
    bases = numbers([(1 - side) * width, side * width])
    whole = pl.BlockSpec(memory_space=pltpu.VMEM)
    return pl.pallas_call(
        functools.partial(finish_kernel, len(mine)),
        in_specs=[SMEM] + [whole] * (1 + len(mine) + len(sums)),
        out_specs=whole,
        out_shape=jax.ShapeDtypeStruct((tok_rows, model), jnp.bfloat16),
        compiler_params=pltpu.CompilerParams(vmem_limit_bytes=16 * 1024 * 1024),
    )(bases, own_gates, *mine, *sums)


def solution(mesh):
    placed = (
        P(("dp", "expert"), None),
        P(("dp", "expert"), None),
        P(("dp", "expert"), None),
        P(),
        P("expert", "dp", None),
        P("expert", "dp", None),
        P("expert", None, "dp"),
    )
    return jax.shard_map(
        shards, mesh=mesh, in_specs=placed, out_specs=P(("dp", "expert"), None), check_vma=False
    )
```
